32 devices in a mesh: groups: 2 (over x), ty: 16 (over z, y, core).
Axes of the slice: x: 2, y: 2, z: 4, core: 2. Of those that a mesh axis runs over, the one named last changes fastest.
Arguments:
- transmission: bfloat16 [4, 2, 8192, 1024], P(None, None, ('groups', 'ty')), parts along dimension 2, may hold values from -4 to 4
- probe_wavefield: float32 [4, 128, 128], P('groups'), parts along dimension 0, may hold values from -6 to 6
- phase_shift: float32 [128, 128], replicated, may hold values from -3.140625 to 3.140625
- offsets: int32 [2, 256], P(None, ('groups', 'ty')), parts along dimension 1, may hold values from 0 to 3968, as said below
- live_counts: int32 [32], P('groups'), parts along dimension 0, may hold values from 0 to 8, as said below
- measured: bfloat16 [256, 128, 128], P(('groups', 'ty')), parts along dimension 0, may hold values from 1 to 9, as said below
Outputs:
- object_grad: float32 [4, 2, 8192, 1024], P(None, None, ('groups', 'ty')), parts along dimension 2
- probe_grad: float32 [4, 128, 128], P('groups'), parts along dimension 0
The draws below stay inside these ranges and needn't reach their ends.
There are 2 independent parts, one for each index of `groups`. The reference program is written for one: setup_inputs(seed, part) draws one part's arguments, and reference() takes and returns one part's arrays. A program takes and returns all parts, laid end to end along the dimension named above; an argument that names none is the same for every part. Nothing has to cross between parts.
Inputs may be any that keep to these rules, and one draw needn't show every extreme that they name: Slot p belongs to device p // 8 along ty; its row offset lies within that device's 256 tile rows and its window stays inside the object; column offsets run from 0 to 896. `live_counts`: the live slots of a device are its first ones; on each aligned pair of devices 2k and 2k+1 along ty the two counts add up to 8. `measured`: positive amplitudes.
All inputs are finite; a program needn't handle non-finite values.
Results may differ from the reference program's by a relative error of at most 0.03.
The reference program's roundings to bfloat16 on the way (of `dft_tables`) count: a program that leaves them out, or rounds other values in their place, can miss the bound.
Values may be sent and summed in bfloat16 or wider, within the bound.
No kernel may reach another device: no remote copies, remote signals or barrier semaphores. Data moves between devices by JAX's collectives and lax.ppermute only.
A program may use at most 128 MiB of HBM per device.

```python
import math
import jax
import jax.numpy as jnp
from jax import lax

SLICES = 4
PATCH = 128
TILE = 256
CAP = 8
NR = 4096
NC = 1024
NPOS = 128
N_TY = 16


def draw_offsets(key, part):
    key = jax.random.fold_in(key, 7)
    row_key, col_key = jax.random.split(key)
    slot_ids = jnp.arange(NPOS, dtype=jnp.int32)
    base_rows = slot_ids // CAP * TILE
    row_shift = jax.random.randint(row_key, (NPOS,), 0, TILE)
    row_shift = jnp.where(slot_ids == 0, TILE - 1, jnp.where(slot_ids == NPOS - CAP, TILE - 1, row_shift))
    limits = jnp.where(base_rows + TILE >= NR, TILE - PATCH, TILE - 1)
    row_offsets = base_rows + jnp.minimum(row_shift, limits)
    col_offsets = jax.random.randint(col_key, (NPOS,), 0, NC - PATCH + 1)
    return jnp.stack([row_offsets, col_offsets], 0).astype(jnp.int32)


def draw_live_counts(key, part):
    key = jax.random.fold_in(key, 11)
    first_counts = jax.random.randint(key, (N_TY // 2,), 0, CAP + 1)
    first_counts = first_counts.at[0].set(CAP // 2)
    first_counts = first_counts.at[N_TY // 2 - 1].set(CAP)
    second_counts = CAP - first_counts
    return jnp.stack([first_counts, second_counts], 1).reshape(N_TY).astype(jnp.int32)


def draw_measured(key, part):
    key = jax.random.fold_in(key, 13)
    slot_ids = jnp.arange(NPOS, dtype=jnp.int32)
    level = 2.0 + 4.0 * (slot_ids // CAP).astype(jnp.float32) / (N_TY - 1)
    factor = jax.random.uniform(key, (NPOS, PATCH, PATCH), jnp.float32, 0.5, 1.5)
    return (level[:, None, None] * factor).astype(jnp.bfloat16)


def block_levels(own_key, shape, pieces, low, top_value):
    gain = 1.0
    for axis_at, shards_of in pieces:
        heights = jax.random.uniform(jax.random.fold_in(jax.random.fold_in(own_key, 6), axis_at), (shards_of,), jnp.float32, low / len(pieces), top_value / len(pieces))
        gain = gain * jnp.repeat(jnp.exp(heights), shape[axis_at] // shards_of).reshape((-1,) + (1,) * (len(shape) - 1 - axis_at))
    return gain


def bell_draw(key, dims, scale, reach, cuts=(), kind=jnp.bfloat16):
    level = block_levels(key, dims, cuts, -0.22, 0.18) if cuts else 1.0
    values = jax.random.normal(key, dims, jnp.float32) * scale * level
    return jnp.minimum(jnp.maximum(values, -reach), reach).astype(kind)


def setup_inputs(seed: int = 0, part: int = 0) -> dict:
    seeds = jax.random.split(jax.random.key(seed), 7)
    part_splits = jax.random.split(jax.random.fold_in(seeds[6], part), 7)
    return {
        "transmission": bell_draw(part_splits[0], (SLICES, 2, NR, NC), 0.7, 4.0, ((2, 16),)),
        "probe_wavefield": bell_draw(part_splits[1], (2, PATCH, PATCH), 1.0, 6.0, (), jnp.float32),
        "phase_shift": jnp.clip(jax.random.uniform(seeds[2], (PATCH, PATCH), jnp.float32, -3.140625, 3.140625), -3.140625, 3.140625),
        "offsets": draw_offsets(jax.random.fold_in(jax.random.fold_in(seeds[6], part), 71), part),
        "live_counts": draw_live_counts(jax.random.fold_in(jax.random.fold_in(seeds[6], part), 71), part),
        "measured": draw_measured(jax.random.fold_in(jax.random.fold_in(seeds[6], part), 71), part),
    }


RIDGE = 0.25

def dft_tables(patch_size, sign):
    positions = jnp.arange(patch_size, dtype=jnp.int32)
    product = positions[:, None] * positions[None, :] % patch_size
    angles = 2.0 * math.pi / patch_size * product.astype(jnp.float32)
    normalizer = 1.0 / math.sqrt(patch_size)
    table_real = jnp.cos(angles) * normalizer
    table_imag = sign * jnp.sin(angles) * normalizer
    left_table = jnp.concatenate([jnp.concatenate([table_real, -table_imag], 1), jnp.concatenate([table_imag, table_real], 1)], 0)
    right_table = jnp.concatenate([jnp.concatenate([table_real, table_imag], 1), jnp.concatenate([-table_imag, table_real], 1)], 0)
    return (left_table.astype(jnp.bfloat16), right_table.astype(jnp.bfloat16))

def transform(wave_real, wave_imag, tables):
    left_table, right_table = tables
    patch_size = wave_real.shape[0]
    stacked = jnp.concatenate([wave_real, wave_imag], 0).astype(jnp.bfloat16)
    halfway = jnp.dot(left_table, stacked, preferred_element_type=jnp.float32).astype(jnp.bfloat16)
    side_by_side = jnp.concatenate([halfway[:patch_size], halfway[patch_size:]], 1)
    result = jnp.dot(side_by_side, right_table, preferred_element_type=jnp.float32)
    return (result[:, :patch_size], result[:, patch_size:])

def position_loss(object_window, probe_wavefield, measured, kernel_real_part, kernel_imaginary, forward_transform, inverse_transform):
    wave_real, wave_imag = (probe_wavefield[0], probe_wavefield[1])
    slices = object_window.shape[0]
    for slice_id in range(slices):
        layer_real, layer_imag = (object_window[slice_id, 0], object_window[slice_id, 1])
        wave_real, wave_imag = (wave_real * layer_real - wave_imag * layer_imag, wave_real * layer_imag + wave_imag * layer_real)
        if slice_id + 1 < slices:
            freq_real, freq_imag = transform(wave_real, wave_imag, forward_transform)
            freq_real, freq_imag = (freq_real * kernel_real_part - freq_imag * kernel_imaginary, freq_real * kernel_imaginary + freq_imag * kernel_real_part)
            wave_real, wave_imag = transform(freq_real, freq_imag, inverse_transform)
    far_real, far_imag = transform(wave_real, wave_imag, forward_transform)
    amplitude = jnp.sqrt(far_real * far_real + far_imag * far_imag + RIDGE)
    return jnp.sum((amplitude - measured.astype(jnp.float32)) ** 2)

def reference(transmission, probe_wavefield, phase_shift, offsets, live_counts, measured):
    patch_size = probe_wavefield.shape[-1]
    forward_transform = dft_tables(patch_size, -1.0)
    inverse_transform = dft_tables(patch_size, 1.0)
    kernel_real_part = jnp.cos(phase_shift)
    kernel_imaginary = jnp.sin(phase_shift)
    positions = offsets.shape[1]
    slot_ids = jnp.arange(positions, dtype=jnp.int32)
    owners = slot_ids // CAP
    weights = (slot_ids % CAP < live_counts[owners]).astype(jnp.float32)
    zero_index = jnp.zeros((), jnp.int32)
    gradient_function = jax.grad(position_loss, argnums=(0, 1))

    def per_position(packed_arrays):
        single_row, single_column, single_weight, single_measurement = packed_arrays
        object_window = lax.dynamic_slice(transmission, (zero_index, zero_index, single_row.astype(jnp.int32), single_column.astype(jnp.int32)), (SLICES, 2, patch_size, patch_size)).astype(jnp.float32)
        window_gradient, probe_gradient = gradient_function(object_window, probe_wavefield, single_measurement, kernel_real_part, kernel_imaginary, forward_transform, inverse_transform)
        return (window_gradient * single_weight, probe_gradient * single_weight)
    g_windows, g_probes = lax.map(per_position, (offsets[0], offsets[1], weights, measured))

    def deposit(slot_id, accumulated):
        corner = (zero_index, zero_index, offsets[0, slot_id].astype(jnp.int32), offsets[1, slot_id].astype(jnp.int32))
        current = lax.dynamic_slice(accumulated, corner, (SLICES, 2, patch_size, patch_size))
        return lax.dynamic_update_slice(accumulated, current + g_windows[slot_id], corner)
    object_grad = lax.fori_loop(0, positions, deposit, jnp.zeros(transmission.shape, jnp.float32))
    probe_grad = lax.optimization_barrier(jnp.sum(g_probes, 0)) / math.sqrt(CAP * N_TY)
    return (object_grad, probe_grad)
```

```python
import math

import jax
import jax.numpy as jnp
import numpy as np
from jax import lax
from jax.experimental import pallas as pl
from jax.experimental.pallas import tpu as pltpu
from jax.sharding import PartitionSpec as P

RIDGE = 0.25
GROUP = 4
LANES = 128


def passed_along(block, axis, distance):
    devices = range(lax.axis_size(axis))
    route = [(i - distance, i) for i in devices if i - distance in devices]
    return lax.ppermute(block, axis, route)


def summed_over(block, axis):
    devices = lax.axis_size(axis)
    if devices & (devices - 1):
        return lax.psum(block, axis)
    step = 1
    while step < devices:
        route = [(i, i ^ step) for i in range(devices)]
        block = block.astype(jnp.bfloat16)
        other = lax.ppermute(block, axis, route)
        block = block.astype(jnp.float32) + other.astype(jnp.float32)
        step *= 2
    return block


def dft_tables(patch_size):
    positions = np.arange(patch_size)
    product = positions[:, None] * positions[None, :] % patch_size
    angles = 2.0 * math.pi / patch_size * product
    real = np.cos(angles) / math.sqrt(patch_size)
    imag = -np.sin(angles) / math.sqrt(patch_size)
    left = np.block([[real, -imag], [imag, real]])
    return (jnp.asarray(left, jnp.bfloat16), jnp.asarray(left.T, jnp.bfloat16))


def matmul(a, b):
    return jnp.dot(a, b, preferred_element_type=jnp.float32)


def swap_halves(block, n):
    return jnp.concatenate(
        [
            jnp.concatenate([block[:n, :n], block[n:, :n]], 1),
            jnp.concatenate([block[:n, n:], block[n:, n:]], 1),
        ],
        0,
    )


def transform_pairs(fields, left, right):
    out = []
    for k in range(0, len(fields), 2):
        (a_re, a_im), (b_re, b_im) = fields[k], fields[k + 1]
        n = a_re.shape[0]
        stacked = jnp.concatenate(
            [
                jnp.concatenate([a_re, a_im], 0).astype(jnp.bfloat16),
                jnp.concatenate([b_re, b_im], 0).astype(jnp.bfloat16),
            ],
            1,
        )
        halfway = matmul(left, stacked).astype(jnp.bfloat16)
        result = matmul(swap_halves(halfway, n), right)
        out += [(result[:n, :n], result[:n, n:]), (result[n:, :n], result[n:, n:])]
    return out


def transform_pairs_back(grads, left, right):
    out = []
    for k in range(0, len(grads), 2):
        (a_re, a_im), (b_re, b_im) = grads[k], grads[k + 1]
        n = a_re.shape[0]
        side = jnp.concatenate(
            [
                jnp.concatenate([a_re, a_im], 1).astype(jnp.bfloat16),
                jnp.concatenate([b_re, b_im], 1).astype(jnp.bfloat16),
            ],
            0,
        )
        halfway = matmul(side, right).astype(jnp.bfloat16)
        stacked = jnp.concatenate(
            [
                jnp.concatenate([halfway[:n, :n], halfway[:n, n:]], 0),
                jnp.concatenate([halfway[n:, :n], halfway[n:, n:]], 0),
            ],
            1,
        )
        result = matmul(left, stacked).astype(jnp.bfloat16).astype(jnp.float32)
        out += [(result[:n, :n], result[n:, :n]), (result[:n, n:], result[n:, n:])]
    return out


def main_kernel(
    row_ref, col_ref, live_ref,
    tile_ref, rim_ref, probe_ref, cos_ref, sin_ref, fwd_ref, bwd_ref, measured_ref,
    object_ref, rim_out_ref, probe_out_ref,
    ext, acc, slab, win, waves, sems,
):
    planes, tile_rows, width = tile_ref.shape
    n = probe_ref.shape[-1]
    blocks = width // LANES
    slices = planes // 2
    capacity = measured_ref.shape[0]
    live = live_ref[0]

    loads = []
    for b in range(blocks):
        cols = pl.ds(b * LANES, LANES)
        loads.append(
            pltpu.make_async_copy(
                tile_ref.at[:, :, cols], ext.at[:, b, pl.ds(0, tile_rows), :], sems.at[2 * b]
            )
        )
        loads.append(
            pltpu.make_async_copy(
                rim_ref.at[:, :, cols], ext.at[:, b, pl.ds(tile_rows, n), :], sems.at[2 * b + 1]
            )
        )
    for load in loads:
        load.start()

    probe_out_ref[...] = jnp.zeros_like(probe_out_ref)

    @pl.loop(0, planes)
    def _(p):
        @pl.loop(0, blocks)
        def _(b):
            acc[p, b] = jnp.zeros(acc.shape[2:], jnp.float32)

    for load in loads:
        load.wait()

    lane = lax.broadcasted_iota(jnp.int32, (n, LANES), 1)
    lane_slab = lax.broadcasted_iota(jnp.int32, (n + 16, LANES), 1)

    def place(slot):
        row = row_ref[slot]
        col = col_ref[slot]
        block = jnp.minimum(col // LANES, blocks - 2)
        return row, block, col - block * LANES

    def cut(k, slot):
        row, block, shift = place(slot)
        base = pl.multiple_of(row // 16 * 16, 16)
        back = lax.rem(LANES - shift, LANES)

        @pl.loop(0, planes)
        def _(p):
            left = ext[p, block, pl.ds(base, n + 16), :].astype(jnp.float32)
            right = ext[p, block + 1, pl.ds(base, n + 16), :].astype(jnp.float32)
            left = pltpu.roll(left, back, 1)
            right = pltpu.roll(right, back, 1)
            slab[...] = jnp.where(lane_slab < LANES - shift, left, right)
            win[k, p] = slab[pl.ds(row - base, n), :]

    def deposit(k, slot):
        row, block, shift = place(slot)
        ahead = lax.rem(shift, LANES)

        @pl.loop(0, planes)
        def _(p):
            grad = pltpu.roll(win[k, p], ahead, 1)
            rows = pl.ds(row, n)
            acc[p, block, rows, :] += jnp.where(lane >= shift, grad, 0.0)
            acc[p, block + 1, rows, :] += jnp.where(lane < shift, grad, 0.0)

    @pl.loop(0, (live + GROUP - 1) // GROUP)
    def _(g):
        slots = [jnp.minimum(g * GROUP + k, capacity - 1) for k in range(GROUP)]
        for k in range(GROUP):
            cut(k, slots[k])
        ahead, behind = fwd_ref[...], bwd_ref[...]
        fields = [(probe_ref[0], probe_ref[1])] * GROUP
        for s in range(slices):
            for k in range(GROUP):
                w_re, w_im = fields[k]
                if s:
                    waves[k, s - 1, 0] = w_re
                    waves[k, s - 1, 1] = w_im
                o_re, o_im = win[k, 2 * s], win[k, 2 * s + 1]
                fields[k] = (w_re * o_re - w_im * o_im, w_re * o_im + w_im * o_re)
            fields = transform_pairs(fields, ahead, behind)
            if s + 1 < slices:
                h_re, h_im = cos_ref[...], sin_ref[...]
                fields = [(a * h_re - b * h_im, a * h_im + b * h_re) for a, b in fields]
                fields = transform_pairs(fields, behind, ahead)
        for k in range(GROUP):
            f_re, f_im = fields[k]
            weight = jnp.where(g * GROUP + k < live, 2.0, 0.0)
            target = measured_ref[slots[k]].astype(jnp.float32)
            inverse = lax.rsqrt(f_re * f_re + f_im * f_im + RIDGE)
            scale = weight * (1.0 - target * inverse)
            fields[k] = (scale * f_re, scale * f_im)
        for s in reversed(range(slices)):
            fields = transform_pairs_back(fields, behind, ahead)
            for k in range(GROUP):
                g_re, g_im = fields[k]
                if s:
                    w_re, w_im = waves[k, s - 1, 0], waves[k, s - 1, 1]
                else:
                    w_re, w_im = probe_ref[0], probe_ref[1]
                o_re, o_im = win[k, 2 * s], win[k, 2 * s + 1]
                fields[k] = (g_re * o_re + g_im * o_im, g_im * o_re - g_re * o_im)
                win[k, 2 * s] = g_re * w_re + g_im * w_im
                win[k, 2 * s + 1] = g_im * w_re - g_re * w_im
            if s:
                fields = transform_pairs_back(fields, ahead, behind)
                h_re, h_im = cos_ref[...], sin_ref[...]
                fields = [(a * h_re + b * h_im, b * h_re - a * h_im) for a, b in fields]
        for part in range(2):
            total = fields[0][part]
            for k in range(1, GROUP):
                total = total + fields[k][part]
            probe_out_ref[part] += total
        for k in range(GROUP):
            @pl.when(g * GROUP + k < live)
            def _():
                deposit(k, slots[k])

    stores = []
    for b in range(blocks):
        stores.append(
            pltpu.make_async_copy(
                acc.at[:, b, pl.ds(0, tile_rows), :],
                object_ref.at[:, :, pl.ds(b * LANES, LANES)],
                sems.at[b],
            )
        )
        stores[-1].start()

    @pl.loop(0, planes)
    def _(p):
        @pl.loop(0, blocks)
        def _(b):
            rim_out_ref[p, b] = acc[p, b, pl.ds(tile_rows, n), :].astype(jnp.bfloat16)

    for store in stores:
        store.wait()


def run_main(row, col, live, tile, rim, probe, h_re, h_im, ahead, behind, measured):
    planes, tile_rows, width = tile.shape
    n = probe.shape[-1]
    blocks = width // LANES
    any_spec = pl.BlockSpec(memory_space=pl.ANY)
    vmem = pl.BlockSpec(memory_space=pltpu.VMEM)
    smem = pl.BlockSpec(memory_space=pltpu.SMEM)
    return pl.pallas_call(
        main_kernel,
        out_shape=(
            jax.ShapeDtypeStruct((planes, tile_rows, width), jnp.float32),
            jax.ShapeDtypeStruct((planes, blocks, n, LANES), jnp.bfloat16),
            jax.ShapeDtypeStruct(probe.shape, jnp.float32),
        ),
        in_specs=[smem] * 3 + [any_spec] * 2 + [vmem] * 6,
        out_specs=(any_spec, vmem, vmem),
        scratch_shapes=[
            pltpu.VMEM((planes, blocks, tile_rows + n, LANES), jnp.bfloat16),
            pltpu.VMEM((planes, blocks, tile_rows + n, LANES), jnp.float32),
            pltpu.VMEM((n + 16, LANES), jnp.float32),
            pltpu.VMEM((GROUP, planes, n, n), jnp.float32),
            pltpu.VMEM((GROUP, planes // 2 - 1, 2, n, n), jnp.float32),
            pltpu.SemaphoreType.DMA((2 * blocks,)),
        ],
        compiler_params=pltpu.CompilerParams(vmem_limit_bytes=48 * 2**20),
    )(row, col, live, tile, rim, probe, h_re, h_im, ahead, behind, measured)


def add_kernel(grad_ref, rim_ref, out_ref):
    for b in range(rim_ref.shape[1]):
        cols = pl.ds(b * LANES, LANES)
        out_ref[0, :, cols] = grad_ref[0, :, cols] + rim_ref[0, b].astype(jnp.float32)


def add_rim(grad, rim):
    planes, _, width = grad.shape
    _, blocks, n, lanes = rim.shape
    block = pl.BlockSpec((1, n, width), lambda p: (p, 0, 0))
    return pl.pallas_call(
        add_kernel,
        grid=(planes,),
        out_shape=jax.ShapeDtypeStruct(grad.shape, grad.dtype),
        in_specs=[block, pl.BlockSpec((1, blocks, n, lanes), lambda p: (p, 0, 0, 0))],
        out_specs=block,
        input_output_aliases={0: 0},
        compiler_params=pltpu.CompilerParams(vmem_limit_bytes=16 * 2**20),
    )(grad, rim)


def local(transmission, probe_wavefield, phase_shift, offsets, live_counts, measured):
    slices, parts, tile_rows, width = transmission.shape
    n = probe_wavefield.shape[-1]
    capacity = offsets.shape[1]
    devices = lax.axis_size("ty")
    my_index = lax.axis_index("ty")
    tile = transmission.reshape(slices * parts, tile_rows, width)
    rim = passed_along(tile[:, :n, :], "ty", -1)
    ahead, behind = dft_tables(n)
    row = offsets[0] - my_index * tile_rows
    live = lax.dynamic_slice(live_counts, (my_index,), (1,))
    grad, rim_out, probe_part = run_main(
        row, offsets[1], live, tile, rim,
        probe_wavefield, jnp.cos(phase_shift), jnp.sin(phase_shift), ahead, behind, measured,
    )
    incoming = passed_along(rim_out, "ty", 1)
    probe_grad = summed_over(probe_part / math.sqrt(capacity * devices), "ty")
    grad = add_rim(grad, incoming)
    return (grad.reshape(slices, parts, tile_rows, width), probe_grad)


def solution(mesh):
    in_specs = (
        P(None, None, ("groups", "ty"), None),
        P("groups", None, None),
        P(),
        P(None, ("groups", "ty")),
        P("groups"),
        P(("groups", "ty"), None, None),
    )
    out_specs = (P(None, None, ("groups", "ty"), None), P("groups", None, None))
    return jax.shard_map(local, mesh=mesh, in_specs=in_specs, out_specs=out_specs, check_vma=False)
```

```python
import functools
import math

import jax
import jax.numpy as jnp
import numpy as np
from jax import lax
from jax.experimental import pallas as pl
from jax.experimental.pallas import tpu as pltpu
from jax.sharding import PartitionSpec as P

RIDGE = 0.25
LANES = 128
CHUNK = 16
PIECE = 8
AXIS = "ty"

ANY = pl.BlockSpec(memory_space=pl.ANY)
VMEM = pl.BlockSpec(memory_space=pltpu.VMEM)
SMEM = pl.BlockSpec(memory_space=pltpu.SMEM)


def params(mib):
    return pltpu.CompilerParams(vmem_limit_bytes=mib * 2**20)


def matmul(a, b):
    return jnp.dot(a, b, preferred_element_type=jnp.float32)


def within_pair(block, up):
    devices = lax.axis_size(AXIS)
    pairs = [(i + 1, i) for i in range(0, devices - 1, 2)]
    if up:
        pairs = [(b, a) for a, b in pairs]
    return lax.ppermute(block, AXIS, pairs)


def between_pairs(block, up):
    devices = lax.axis_size(AXIS)
    pairs = [(i + 1, i) for i in range(1, devices - 1, 2)]
    if up:
        pairs = [(b, a) for a, b in pairs]
    return lax.ppermute(block, AXIS, pairs)


def between_pairs_upto(level, packed, up, beside, operands):
    chunks = packed.shape[0]
    pieces = (chunks - LANES // CHUNK) // PIECE

    def branch(pieces_sent):
        def run(packed, *operands):
            if pieces_sent == 0:
                return packed, beside(*operands)
            sent = PIECE * pieces_sent
            got = between_pairs(packed[:sent], up)
            other = beside(*operands)
            if sent < chunks:
                rest = jnp.zeros((chunks - sent,) + packed.shape[1:], packed.dtype)
                got = jnp.concatenate([got, rest], 0)
            return got, other

        return run

    return lax.switch(level, [branch(i) for i in range(pieces + 1)], packed, *operands)


def summed_over(block, rounds):
    for steps in rounds:
        block = block.astype(jnp.bfloat16)
        devices = lax.axis_size(AXIS)
        got = [lax.ppermute(block, AXIS, [(i, i ^ s) for i in range(devices)]) for s in steps]
        terms = [t.astype(jnp.float32) for t in [block] + got]
        if len(terms) == 2:
            block = terms[0] + terms[1]
        else:
            block = (terms[0] + terms[1]) + (terms[2] + terms[3])
    return block


def exchange_rounds(devices):
    rounds = []
    step = 1
    while step < devices:
        if step * 2 < devices:
            rounds.append((step, 2 * step, 3 * step))
        else:
            rounds.append((step,))
        step *= 4
    return rounds[::-1]


def place(offsets_ref, slot, blocks):
    col = offsets_ref[1, slot]
    block = jnp.minimum(col // LANES, blocks - 2)
    return block, col - block * LANES


def rows_below(offsets_ref, slot, owner, tile_rows, n):
    below = jnp.maximum(offsets_ref[0, slot] - owner * tile_rows + n - tile_rows, 0)
    return below, (below + CHUNK - 1) // CHUNK


def selector(shift, transposed):
    shape = (LANES, 2 * LANES) if transposed else (2 * LANES, LANES)
    wide = lax.broadcasted_iota(jnp.int32, shape, 1 if transposed else 0)
    narrow = lax.broadcasted_iota(jnp.int32, shape, 0 if transposed else 1)
    return jnp.where(wide == narrow + shift, 1.0, 0.0).astype(jnp.bfloat16)


def pack_kernel(own_ref, prev_ref, live_ref, tile_ref, packed_ref, level_ref, buf, sems):
    planes, tile_rows, width = tile_ref.shape
    n = buf.shape[2]
    blocks = width // LANES
    capacity = own_ref.shape[1]
    me = lax.axis_index(AXIS)
    before = jnp.maximum(me - 1, 0)
    live_before = jnp.where(me > 0, live_ref[before], 0)
    live_own = live_ref[me]

    def needs(slot):
        below, chunks = rows_below(prev_ref, slot, before, tile_rows, n)
        return jnp.where(slot < live_before, chunks, 0)

    def load(slot):
        block, _ = place(prev_ref, slot, blocks)
        cols = pl.ds(pl.multiple_of(block * LANES, LANES), 2 * LANES)
        return pltpu.make_async_copy(
            tile_ref.at[:, pl.ds(0, n), cols], buf.at[slot], sems.at[slot]
        )

    for slot in range(capacity):
        @pl.when(needs(slot) > 0)
        def _():
            load(slot).start()

    total_own = 0
    for slot in range(capacity):
        _, chunks = rows_below(own_ref, slot, me, tile_rows, n)
        total_own += jnp.where(slot < live_own, chunks, 0)

    def pack(slot, first):
        chunks = needs(slot)

        @pl.when(chunks > 0)
        def _():
            load(slot).wait()
            _, shift = place(prev_ref, slot, blocks)
            table = selector(shift, False)
            for p in range(planes):
                rows = matmul(buf[slot, p], table).astype(jnp.bfloat16)
                for c in range(n // CHUNK):
                    packed_ref[first + c, p] = rows[c * CHUNK : (c + 1) * CHUNK]

        return first + chunks

    total_before = lax.fori_loop(0, live_before, pack, 0)
    total = jnp.where(me % 2 == 1, total_own, total_before)
    level_ref[0] = (total + PIECE - 1) // PIECE


def pack(own, prev, live_counts, tile, n):
    planes = tile.shape[0]
    capacity = own.shape[1]
    chunks = capacity * (n // CHUNK)
    return pl.pallas_call(
        pack_kernel,
        out_shape=(
            jax.ShapeDtypeStruct((chunks + n // CHUNK, planes, CHUNK, LANES), jnp.bfloat16),
            jax.ShapeDtypeStruct((1,), jnp.int32),
        ),
        in_specs=[SMEM, SMEM, SMEM, ANY],
        out_specs=(VMEM, SMEM),
        scratch_shapes=[
            pltpu.VMEM((capacity, planes, n, 2 * LANES), jnp.bfloat16),
            pltpu.SemaphoreType.DMA((capacity,)),
        ],
        compiler_params=params(20),
        name="pack_rows",
    )(own, prev, live_counts, tile)


def cut_kernel(own_ref, live_ref, tile_ref, win_ref, buf, slab, sems):
    planes, tile_rows, width = tile_ref.shape
    n = win_ref.shape[2]
    blocks = width // LANES
    capacity = own_ref.shape[1]
    tall = buf.shape[2]
    me = lax.axis_index(AXIS)
    live = live_ref[me]

    def top(slot):
        row = own_ref[0, slot] - me * tile_rows
        base = jnp.minimum(row // CHUNK * CHUNK, tile_rows - tall)
        return pl.multiple_of(base, CHUNK), row - base

    def load(slot):
        block, _ = place(own_ref, slot, blocks)
        cols = pl.ds(pl.multiple_of(block * LANES, LANES), 2 * LANES)
        base, _ = top(slot)
        return pltpu.make_async_copy(
            tile_ref.at[:, pl.ds(base, tall), cols], buf.at[slot], sems.at[slot]
        )

    for slot in range(capacity):
        @pl.when(slot < live)
        def _():
            load(slot).start()

    for p in range(planes):
        slab[p, pl.ds(tall, n), :] = jnp.zeros((n, LANES), jnp.float32)

    @pl.loop(0, capacity)
    def _(slot):
        @pl.when(slot < live)
        def _():
            load(slot).wait()
            _, shift = place(own_ref, slot, blocks)
            _, skip = top(slot)
            table = selector(shift, False)
            for p in range(planes):
                slab[p, pl.ds(0, tall), :] = matmul(buf[slot, p], table)
            for p in range(planes):
                win_ref[slot, p] = slab[p, pl.ds(skip, n), :].astype(jnp.bfloat16)

        @pl.when(slot >= live)
        def _():
            win_ref[slot] = jnp.zeros(win_ref.shape[1:], jnp.bfloat16)


def cut(own, live_counts, tile, n):
    planes = tile.shape[0]
    capacity = own.shape[1]
    tall = n + CHUNK
    return pl.pallas_call(
        cut_kernel,
        out_shape=jax.ShapeDtypeStruct((capacity, planes, n, LANES), jnp.bfloat16),
        in_specs=[SMEM, SMEM, ANY],
        out_specs=VMEM,
        scratch_shapes=[
            pltpu.VMEM((capacity, planes, tall, 2 * LANES), jnp.bfloat16),
            pltpu.VMEM((planes, tall + n, LANES), jnp.float32),
            pltpu.SemaphoreType.DMA((capacity,)),
        ],
        compiler_params=params(20),
        cost_estimate=pl.CostEstimate(flops=10**9, bytes_accessed=10**7, transcendentals=0),
        name="cut_windows",
    )(own, live_counts, tile)


def dft_tables(n):
    positions = np.arange(n)
    product = positions[:, None] * positions[None, :] % n
    angles = 2.0 * math.pi / n * product
    real = np.cos(angles) / math.sqrt(n)
    imag = -np.sin(angles) / math.sqrt(n)
    left = np.block([[real, -imag], [imag, real]])
    return (jnp.asarray(left, jnp.bfloat16), jnp.asarray(left.T, jnp.bfloat16))


def stack_rows(fields):
    return jnp.concatenate(
        [jnp.concatenate([re, im], 0).astype(jnp.bfloat16) for re, im in fields], 1
    )


def stack_lanes(fields):
    return jnp.concatenate(
        [jnp.concatenate([re, im], 1).astype(jnp.bfloat16) for re, im in fields], 0
    )


def from_rows(block, n):
    return [(block[:n, k * n : (k + 1) * n], block[n:, k * n : (k + 1) * n]) for k in range(2)]


def from_lanes(block, n):
    return [(block[k * n : (k + 1) * n, :n], block[k * n : (k + 1) * n, n:]) for k in range(2)]


def transform(fields, left, right):
    n = fields[0][0].shape[0]
    out = []
    halfway = [matmul(left, stack_rows(fields[k : k + 2])) for k in range(0, len(fields), 2)]
    for half in halfway:
        out += from_lanes(matmul(stack_lanes(from_rows(half, n)), right), n)
    return out


def transform_back(grads, left, right):
    n = grads[0][0].shape[0]
    out = []
    halfway = [matmul(stack_lanes(grads[k : k + 2]), right) for k in range(0, len(grads), 2)]
    for half in halfway:
        result = matmul(left, stack_rows(from_lanes(half, n)))
        out += from_rows(result.astype(jnp.bfloat16).astype(jnp.float32), n)
    return out


def wave_kernel(
    scale, tile_rows,
    own_ref, live_ref, pair_ref, cross_ref, win_ref,
    probe_ref, cos_ref, sin_ref, fwd_ref, bwd_ref, measured_ref,
    packed_ref, grads_ref, probe_out_ref,
    below_ref, win, waves, sems,
):
    capacity, planes, n, _ = win_ref.shape
    slices = planes // 2
    me = lax.axis_index(AXIS)
    live = live_ref[me]
    odd = me % 2 == 1
    pieces = below_ref.shape[0] // PIECE

    def needs(slot):
        below, chunks = rows_below(own_ref, slot, me, tile_rows, n)
        return below, jnp.where(slot < live, chunks, 0)

    total = 0
    for slot in range(capacity):
        total += needs(slot)[1]

    def load(source, piece):
        part = pl.ds(piece * PIECE, PIECE)
        return pltpu.make_async_copy(source.at[part], below_ref.at[part], sems.at[piece])

    for piece in range(pieces):
        @pl.when((piece * PIECE < total) & odd)
        def _():
            load(cross_ref, piece).start()

        @pl.when((piece * PIECE < total) & jnp.logical_not(odd))
        def _():
            load(pair_ref, piece).start()

    @pl.loop(0, capacity)
    def _(slot):
        for p in range(planes):
            win[slot, p, pl.ds(0, n), :] = win_ref[slot, p].astype(jnp.float32)

    for piece in range(pieces):
        @pl.when(piece * PIECE < total)
        def _():
            load(pair_ref, piece).wait()

    def fill(slot, first):
        below, chunks = needs(slot)

        @pl.loop(0, chunks)
        def _(c):
            for p in range(planes):
                win[slot, p, pl.ds(n - below + c * CHUNK, CHUNK), :] = below_ref[
                    first + c, p
                ].astype(jnp.float32)

        return first + chunks

    lax.fori_loop(0, live, fill, 0)

    def run(count):
        ahead, behind = fwd_ref[...], bwd_ref[...]
        fields = [(probe_ref[0], probe_ref[1])] * count
        for s in range(slices):
            for k in range(count):
                w_re, w_im = fields[k]
                if s:
                    waves[k, s - 1, 0] = w_re
                    waves[k, s - 1, 1] = w_im
                o_re, o_im = win[k, 2 * s, :n, :], win[k, 2 * s + 1, :n, :]
                fields[k] = (w_re * o_re - w_im * o_im, w_re * o_im + w_im * o_re)
            fields = transform(fields, ahead, behind)
            if s + 1 < slices:
                h_re, h_im = cos_ref[...], sin_ref[...]
                fields = [(a * h_re - b * h_im, a * h_im + b * h_re) for a, b in fields]
                fields = transform(fields, behind, ahead)
        for k in range(count):
            f_re, f_im = fields[k]
            weight = jnp.where(k < live, 2.0, 0.0)
            target = measured_ref[k].astype(jnp.float32)
            inverse = lax.rsqrt(f_re * f_re + f_im * f_im + RIDGE)
            slope = weight * (1.0 - target * inverse)
            fields[k] = (slope * f_re, slope * f_im)
        for s in reversed(range(slices)):
            fields = transform_back(fields, behind, ahead)
            for k in range(count):
                g_re, g_im = fields[k]
                if s:
                    w_re, w_im = waves[k, s - 1, 0], waves[k, s - 1, 1]
                else:
                    w_re, w_im = probe_ref[0], probe_ref[1]
                o_re, o_im = win[k, 2 * s, :n, :], win[k, 2 * s + 1, :n, :]
                fields[k] = (g_re * o_re + g_im * o_im, g_im * o_re - g_re * o_im)
                d_re = g_re * w_re + g_im * w_im
                d_im = g_im * w_re - g_re * w_im
                win[k, 2 * s, :n, :] = d_re
                win[k, 2 * s + 1, :n, :] = d_im
                grads_ref[k, 2 * s] = d_re.astype(jnp.bfloat16)
                grads_ref[k, 2 * s + 1] = d_im.astype(jnp.bfloat16)
            if s:
                fields = transform_back(fields, ahead, behind)
                h_re, h_im = cos_ref[...], sin_ref[...]
                fields = [(a * h_re + b * h_im, b * h_re - a * h_im) for a, b in fields]
        for part in range(2):
            total = fields[0][part]
            for k in range(1, count):
                total = total + fields[k][part]
            probe_out_ref[part] = (total * scale).astype(jnp.bfloat16)

    half = capacity // 2

    @pl.when(live > half)
    def _():
        run(capacity)

    @pl.when(live <= half)
    def _():
        run(half)

    def hand_on(slot, first):
        below, chunks = needs(slot)

        @pl.when(chunks > 0)
        def _():
            for p in range(planes):
                win[slot, p, pl.ds(n, CHUNK), :] = jnp.zeros((CHUNK, LANES), jnp.float32)

        @pl.loop(0, chunks)
        def _(c):
            for p in range(planes):
                packed_ref[first + c, p] = win[
                    slot, p, pl.ds(n - below + c * CHUNK, CHUNK), :
                ].astype(jnp.bfloat16)

        return first + chunks

    lax.fori_loop(0, live, hand_on, 0)


def run_waves(scale, tile_rows, own, live_counts, from_pair, from_cross, win, probe, h_re, h_im, tables, measured):
    capacity, planes, n, _ = win.shape
    chunks = from_pair.shape[0]
    return pl.pallas_call(
        functools.partial(wave_kernel, scale, tile_rows),
        out_shape=(
            jax.ShapeDtypeStruct((chunks, planes, CHUNK, LANES), jnp.bfloat16),
            jax.ShapeDtypeStruct(win.shape, jnp.bfloat16),
            jax.ShapeDtypeStruct(probe.shape, jnp.bfloat16),
        ),
        in_specs=[SMEM] * 2 + [ANY] * 2 + [VMEM] * 7,
        out_specs=(VMEM,) * 3,
        scratch_shapes=[
            pltpu.VMEM(from_pair.shape, jnp.bfloat16),
            pltpu.VMEM((capacity, planes, n + CHUNK, LANES), jnp.float32),
            pltpu.VMEM((capacity, planes // 2 - 1, 2, n, n), jnp.float32),
            pltpu.SemaphoreType.DMA((chunks // PIECE,)),
        ],
        compiler_params=params(40),
        name="waves",
    )(own, live_counts, from_pair, from_cross, win, probe, h_re, h_im, *tables, measured)


def deposit_kernel(own_ref, live_ref, grads_ref, object_ref, acc, sems):
    capacity, planes, n, _ = grads_ref.shape
    tile_rows = object_ref.shape[1]
    blocks = object_ref.shape[2] // LANES
    me = lax.axis_index(AXIS)

    @pl.loop(0, planes)
    def _(p):
        for b in range(blocks):
            acc[p, b] = jnp.zeros(acc.shape[2:], jnp.float32)

    @pl.loop(0, live_ref[me])
    def _(slot):
        block, shift = place(own_ref, slot, blocks)
        rows = pl.ds(own_ref[0, slot] - me * tile_rows, n)
        table = selector(shift, True)
        for p in range(planes):
            wide = matmul(grads_ref[slot, p], table)
            acc[p, block, rows, :] += wide[:, :LANES]
            acc[p, block + 1, rows, :] += wide[:, LANES:]

    stores = []
    for b in range(blocks):
        stores.append(
            pltpu.make_async_copy(
                acc.at[:, b, pl.ds(0, tile_rows), :],
                object_ref.at[:, :, pl.ds(b * LANES, LANES)],
                sems.at[b],
            )
        )
        stores[-1].start()
    for store in stores:
        store.wait()


def deposit(own, live_counts, grads, tile_rows, width):
    capacity, planes, n, _ = grads.shape
    blocks = width // LANES
    return pl.pallas_call(
        deposit_kernel,
        out_shape=jax.ShapeDtypeStruct((planes, tile_rows, width), jnp.float32),
        in_specs=[SMEM, SMEM, VMEM],
        out_specs=ANY,
        scratch_shapes=[
            pltpu.VMEM((planes, blocks, tile_rows + n, LANES), jnp.float32),
            pltpu.SemaphoreType.DMA((blocks,)),
        ],
        compiler_params=params(20),
        cost_estimate=pl.CostEstimate(flops=10**9, bytes_accessed=10**7, transcendentals=0),
        name="deposit_windows",
    )(own, live_counts, grads)


def finish_kernel(prev_ref, live_ref, object_in_ref, pair_ref, cross_ref, object_ref, back, acc, sems):
    planes, tile_rows, width = object_ref.shape
    blocks = width // LANES
    capacity = prev_ref.shape[1]
    n = acc.shape[2]
    pieces = back.shape[0] // PIECE
    me = lax.axis_index(AXIS)
    odd = me % 2 == 1
    before = jnp.maximum(me - 1, 0)
    live = jnp.where(me > 0, live_ref[before], 0)

    def needs(slot):
        _, chunks = rows_below(prev_ref, slot, before, tile_rows, n)
        return jnp.where(slot < live, chunks, 0)

    total = 0
    touched = [False] * blocks
    for slot in range(capacity):
        chunks = needs(slot)
        block, _ = place(prev_ref, slot, blocks)
        total += chunks
        for b in range(blocks):
            touched[b] |= (chunks > 0) & ((block == b) | (block + 1 == b))

    def load(source, piece):
        part = pl.ds(piece * PIECE, PIECE)
        return pltpu.make_async_copy(source.at[part], back.at[part], sems.at[piece])

    def tile_part(ref, b):
        return ref.at[:, pl.ds(0, n), pl.ds(b * LANES, LANES)]

    for piece in range(pieces):
        @pl.when((piece * PIECE < total) & odd)
        def _():
            load(pair_ref, piece).start()

        @pl.when((piece * PIECE < total) & jnp.logical_not(odd))
        def _():
            load(cross_ref, piece).start()

    def fetch(b):
        return pltpu.make_async_copy(tile_part(object_in_ref, b), acc.at[:, b], sems.at[pieces + b])

    def put(b):
        return pltpu.make_async_copy(acc.at[:, b], tile_part(object_ref, b), sems.at[pieces + b])

    for b in range(blocks):
        pl.when(touched[b])(lambda: fetch(b).start())
    for piece in range(pieces):
        pl.when(piece * PIECE < total)(lambda: load(pair_ref, piece).wait())
    for b in range(blocks):
        pl.when(touched[b])(lambda: fetch(b).wait())

    def add(slot, first):
        chunks = needs(slot)

        @pl.when(chunks > 0)
        def _():
            block, shift = place(prev_ref, slot, blocks)
            table = selector(shift, True)
            for p in range(planes):
                parts = []
                for c in range(n // CHUNK):
                    part = back[first + c, p]
                    parts.append(jnp.where(c < chunks, part, jnp.zeros_like(part)))
                wide = matmul(jnp.concatenate(parts, 0), table)
                acc[p, block] += wide[:, :LANES]
                acc[p, block + 1] += wide[:, LANES:]

        return first + chunks

    lax.fori_loop(0, live, add, 0)

    for b in range(blocks):
        pl.when(touched[b])(lambda: put(b).start())
    for b in range(blocks):
        pl.when(touched[b])(lambda: put(b).wait())


def finish(prev, live_counts, grad, from_pair, from_cross, n):
    planes, _, width = grad.shape
    blocks = width // LANES
    return pl.pallas_call(
        finish_kernel,
        out_shape=jax.ShapeDtypeStruct(grad.shape, grad.dtype),
        in_specs=[SMEM, SMEM, ANY, ANY, ANY],
        out_specs=ANY,
        input_output_aliases={2: 0},
        scratch_shapes=[
            pltpu.VMEM(from_pair.shape, jnp.bfloat16),
            pltpu.VMEM((planes, blocks, n, LANES), jnp.float32),
            pltpu.SemaphoreType.DMA((from_pair.shape[0] // PIECE + blocks,)),
        ],
        compiler_params=params(16),
        name="add_from_before",
    )(prev, live_counts, grad, from_pair, from_cross)


def local(transmission, probe_wavefield, phase_shift, offsets, live_counts, measured):
    slices, parts, tile_rows, width = transmission.shape
    n = probe_wavefield.shape[-1]
    capacity = offsets.shape[1]
    devices = lax.axis_size(AXIS)
    tile = transmission.reshape(slices * parts, tile_rows, width)
    prev = lax.ppermute(offsets, AXIS, [(i, i + 1) for i in range(devices - 1)])
    packed, level = pack(offsets, prev, live_counts, tile, n)
    level = level[0]
    from_pair = within_pair(packed, False)
    from_cross, win = between_pairs_upto(
        level, packed, False,
        lambda own, live, tile: cut(own, live, tile, n),
        (offsets, live_counts, tile),
    )
    scale = 1.0 / math.sqrt(capacity * devices)
    packed_out, grads, probe_part = run_waves(
        scale, tile_rows, offsets, live_counts, from_pair, from_cross, win,
        probe_wavefield, jnp.cos(phase_shift), jnp.sin(phase_shift), dft_tables(n), measured,
    )
    rounds = exchange_rounds(devices)
    back_pair = within_pair(packed_out, True)
    back_cross, grad = between_pairs_upto(
        level, packed_out, True,
        lambda own, live, grads: deposit(own, live, grads, tile_rows, width),
        (offsets, live_counts, grads),
    )
    probe_grad = summed_over(probe_part, rounds)
    grad = finish(prev, live_counts, grad, back_pair, back_cross, n)
    return (grad.reshape(slices, parts, tile_rows, width), probe_grad)


def solution(mesh):
    in_specs = (
        P(None, None, ("groups", "ty"), None),
        P("groups", None, None),
        P(),
        P(None, ("groups", "ty")),
        P("groups"),
        P(("groups", "ty"), None, None),
    )
    out_specs = (P(None, None, ("groups", "ty"), None), P("groups", None, None))
    return jax.shard_map(local, mesh=mesh, in_specs=in_specs, out_specs=out_specs, check_vma=False)
```

```python
import functools
import math

import jax
import jax.numpy as jnp
import numpy as np
from jax import lax
from jax.experimental import pallas as pl
from jax.experimental.pallas import tpu as pltpu
from jax.sharding import PartitionSpec as P

RIDGE = 0.25
LANES = 128
CHUNK = 16
PIECE = 8
AXIS = "ty"

ANY = pl.BlockSpec(memory_space=pl.ANY)
VMEM = pl.BlockSpec(memory_space=pltpu.VMEM)
SMEM = pl.BlockSpec(memory_space=pltpu.SMEM)


def params(mib):
    return pltpu.CompilerParams(vmem_limit_bytes=mib * 2**20)


def matmul(a, b):
    return jnp.dot(a, b, preferred_element_type=jnp.float32)


def within_pair(block, up):
    devices = lax.axis_size(AXIS)
    pairs = [(i + 1, i) for i in range(0, devices - 1, 2)]
    if up:
        pairs = [(b, a) for a, b in pairs]
    return lax.ppermute(block, AXIS, pairs)


def between_pairs(block, up):
    devices = lax.axis_size(AXIS)
    pairs = [(i + 1, i) for i in range(1, devices - 1, 2)]
    if up:
        pairs = [(b, a) for a, b in pairs]
    return lax.ppermute(block, AXIS, pairs)


def level_sizes(chunks):
    return (chunks // 4, 3 * chunks // 8, chunks // 2, chunks)


def level_of(total, sizes):
    level = 0
    for size in sizes[:-1]:
        level += jnp.where(total > size, 1, 0)
    return level


def copy_kernel(rows, source_ref, target_ref, sem):
    if rows is None:
        target = target_ref.at[pl.ds(0, source_ref.shape[0])]
        copy = pltpu.make_async_copy(source_ref, target, sem)
    else:
        copy = pltpu.make_async_copy(source_ref.at[:, pl.ds(0, rows), :], target_ref, sem)
    copy.start()
    copy.wait()


def copied(block, shape, rows=None):
    return pl.pallas_call(
        functools.partial(copy_kernel, rows),
        out_shape=jax.ShapeDtypeStruct(shape, block.dtype),
        in_specs=[ANY],
        out_specs=ANY,
        scratch_shapes=[pltpu.SemaphoreType.DMA],
        compiler_params=params(2),
        name="copy_rows" if rows else "place_chunks",
    )(block)


def between_pairs_upto(level, packed, up, beside, operands):
    full = packed[-1].shape

    def branch(i):
        def run(packed, *operands):
            got = between_pairs(packed[i], up)
            other = beside(*operands)
            if got.shape != full:
                got = copied(got, full)
            return got, other

        return run

    return lax.switch(level, [branch(i) for i in range(len(packed))], packed, *operands)


def sum_kernel(count, *refs):
    terms = [ref[...].astype(jnp.float32) for ref in refs[:count]]
    if count == 2:
        total = terms[0] + terms[1]
    else:
        total = (terms[0] + terms[1]) + (terms[2] + terms[3])
    out_ref = refs[-1]
    out_ref[...] = total.astype(out_ref.dtype)


def exchange(block, steps):
    devices = lax.axis_size(AXIS)
    return [block] + [lax.ppermute(block, AXIS, [(i, i ^ s) for i in range(devices)]) for s in steps]


def summed(terms, dtype, after=()):
    return pl.pallas_call(
        functools.partial(sum_kernel, len(terms)),
        out_shape=jax.ShapeDtypeStruct(terms[0].shape, dtype),
        in_specs=[VMEM] * len(terms) + [ANY] * len(after),
        out_specs=VMEM,
        compiler_params=params(4),
        name="sum_partners",
    )(*terms, *after)


def exchange_rounds(devices):
    rounds = []
    step = 1
    while step < devices:
        if step * 2 < devices:
            rounds.append((step, 2 * step, 3 * step))
        else:
            rounds.append((step,))
        step *= 4
    return rounds[::-1]


def place(offsets_ref, slot, blocks):
    col = offsets_ref[1, slot]
    block = jnp.minimum(col // LANES, blocks - 2)
    return block, col - block * LANES


def rows_below(offsets_ref, slot, owner, tile_rows, n):
    below = jnp.maximum(offsets_ref[0, slot] - owner * tile_rows + n - tile_rows, 0)
    return below, (below + CHUNK - 1) // CHUNK


def selector(shift, transposed):
    shape = (LANES, 2 * LANES) if transposed else (2 * LANES, LANES)
    wide = lax.broadcasted_iota(jnp.int32, shape, 1 if transposed else 0)
    narrow = lax.broadcasted_iota(jnp.int32, shape, 0 if transposed else 1)
    return jnp.where(wide == narrow + shift, 1.0, 0.0).astype(jnp.bfloat16)


def pack_kernel(sizes, own_ref, prev_ref, live_ref, tile_ref, *refs):
    level_ref, *packed_refs, buf, packed, sems = refs[2:]
    planes, tile_rows, width = tile_ref.shape
    n = buf.shape[2]
    blocks = width // LANES
    capacity = own_ref.shape[1]
    me = lax.axis_index(AXIS)
    odd = me % 2 == 1
    before = jnp.maximum(me - 1, 0)
    live_before = jnp.where((me > 0) & jnp.logical_not(odd), live_ref[before], 0)
    live_own = live_ref[me]

    def needs(slot):
        below, chunks = rows_below(prev_ref, slot, before, tile_rows, n)
        return jnp.where(slot < live_before, chunks, 0)

    def load(slot):
        block, _ = place(prev_ref, slot, blocks)
        cols = pl.ds(pl.multiple_of(block * LANES, LANES), 2 * LANES)
        return pltpu.make_async_copy(
            tile_ref.at[:, pl.ds(0, n), cols], buf.at[slot], sems.at[slot]
        )

    @pl.loop(0, live_before)
    def _(slot):
        pl.when(needs(slot) > 0)(load(slot).start)

    total_own = 0
    for slot in range(capacity):
        _, chunks = rows_below(own_ref, slot, me, tile_rows, n)
        total_own += jnp.where(slot < live_own, chunks, 0)

    def pack(slot, first):
        chunks = needs(slot)

        @pl.when(chunks > 0)
        def _():
            load(slot).wait()
            _, shift = place(prev_ref, slot, blocks)
            table = selector(shift, False)
            for p in range(planes):
                rows = matmul(buf[slot, p], table).astype(jnp.bfloat16)
                for c in range(n // CHUNK):
                    packed[first + c, p] = rows[c * CHUNK : (c + 1) * CHUNK]

        return first + chunks

    total_before = lax.fori_loop(0, live_before, pack, 0)
    level = level_of(jnp.where(odd, total_own, total_before), sizes)
    level_ref[0] = level
    for i, size in enumerate(sizes):
        @pl.when((level == i) & (total_before > 0))
        def _():
            store = pltpu.make_async_copy(
                packed.at[pl.ds(0, size)], packed_refs[i], sems.at[capacity]
            )
            store.start()
            store.wait()


def pack(own, prev, live_counts, tile, n, after):
    planes = tile.shape[0]
    capacity = own.shape[1]
    sizes = level_sizes(capacity * (n // CHUNK))
    level, *packed = pl.pallas_call(
        functools.partial(pack_kernel, sizes),
        out_shape=[jax.ShapeDtypeStruct((1,), jnp.int32)]
        + [jax.ShapeDtypeStruct((size, planes, CHUNK, LANES), jnp.bfloat16) for size in sizes],
        in_specs=[SMEM, SMEM, SMEM, ANY] + [ANY] * len(after),
        out_specs=[SMEM] + [ANY] * len(sizes),
        scratch_shapes=[
            pltpu.VMEM((capacity, planes, n, 2 * LANES), jnp.bfloat16),
            pltpu.VMEM((sizes[-1] + n // CHUNK, planes, CHUNK, LANES), jnp.bfloat16),
            pltpu.SemaphoreType.DMA((capacity + 1,)),
        ],
        compiler_params=params(12),
        name="pack_rows",
    )(own, prev, live_counts, tile, *after)
    return level[0], packed


def cut_kernel(own_ref, live_ref, tile_ref, rim_ref, win_ref, buf, slab, sems):
    planes, tile_rows, width = tile_ref.shape
    n = win_ref.shape[2]
    blocks = width // LANES
    capacity = own_ref.shape[1]
    tall = n + CHUNK
    me = lax.axis_index(AXIS)
    live = live_ref[me]

    def top(slot):
        row = own_ref[0, slot] - me * tile_rows
        base = jnp.minimum(row // CHUNK * CHUNK, tile_rows - tall)
        return pl.multiple_of(base, CHUNK), row - base

    def loads(slot):
        block, _ = place(own_ref, slot, blocks)
        cols = pl.ds(pl.multiple_of(block * LANES, LANES), 2 * LANES)
        base, skip = top(slot)
        own = pltpu.make_async_copy(
            tile_ref.at[:, pl.ds(base, tall), cols],
            buf.at[slot, :, pl.ds(0, tall), :],
            sems.at[2 * slot],
        )
        rim = pltpu.make_async_copy(
            rim_ref.at[:, :, cols], buf.at[slot, :, pl.ds(tall, n), :], sems.at[2 * slot + 1]
        )
        return own, rim, (skip > CHUNK) & (me % 2 == 0)

    @pl.loop(0, live)
    def _(slot):
        own, rim, crosses = loads(slot)
        own.start()
        pl.when(crosses)(rim.start)

    @pl.loop(0, capacity)
    def _(slot):
        @pl.when(slot < live)
        def _():
            own, rim, crosses = loads(slot)
            own.wait()
            pl.when(crosses)(rim.wait)
            _, shift = place(own_ref, slot, blocks)
            _, skip = top(slot)
            table = selector(shift, False)

            @pl.loop(0, planes)
            def _(p):
                slab[p] = matmul(buf[slot, p], table)

            @pl.loop(0, planes, unroll=2)
            def _(p):
                win_ref[slot, p] = slab[p, pl.ds(skip, n), :].astype(jnp.bfloat16)

        @pl.when(slot >= live)
        def _():
            @pl.loop(0, planes)
            def _(p):
                win_ref[slot, p] = jnp.zeros(win_ref.shape[2:], jnp.bfloat16)


def cut(own, live_counts, tile, rim):
    planes, n, _ = rim.shape
    capacity = own.shape[1]
    tall = n + CHUNK
    return pl.pallas_call(
        cut_kernel,
        out_shape=jax.ShapeDtypeStruct((capacity, planes, n, LANES), jnp.bfloat16),
        in_specs=[SMEM, SMEM, ANY, ANY],
        out_specs=VMEM,
        scratch_shapes=[
            pltpu.VMEM((capacity, planes, tall + n, 2 * LANES), jnp.bfloat16),
            pltpu.VMEM((planes, tall + n, LANES), jnp.float32),
            pltpu.SemaphoreType.DMA((2 * capacity,)),
        ],
        compiler_params=params(16),
        cost_estimate=pl.CostEstimate(flops=10**9, bytes_accessed=10**7, transcendentals=0),
        name="cut_windows",
    )(own, live_counts, tile, rim)


def dft_tables(n):
    positions = np.arange(n)
    product = positions[:, None] * positions[None, :] % n
    angles = 2.0 * math.pi / n * product
    real = np.cos(angles) / math.sqrt(n)
    imag = -np.sin(angles) / math.sqrt(n)
    left = np.block([[real, -imag], [imag, real]])
    return (jnp.asarray(left, jnp.bfloat16), jnp.asarray(left.T, jnp.bfloat16))


def stack_rows(fields):
    return jnp.concatenate(
        [jnp.concatenate([re, im], 0).astype(jnp.bfloat16) for re, im in fields], 1
    )


def stack_lanes(fields):
    return jnp.concatenate(
        [jnp.concatenate([re, im], 1).astype(jnp.bfloat16) for re, im in fields], 0
    )


def from_rows(block, n):
    return [(block[:n, k * n : (k + 1) * n], block[n:, k * n : (k + 1) * n]) for k in range(2)]


def from_lanes(block, n):
    return [(block[k * n : (k + 1) * n, :n], block[k * n : (k + 1) * n, n:]) for k in range(2)]


def transform(fields, left, right):
    n = fields[0][0].shape[0]
    out = []
    halfway = [matmul(left, stack_rows(fields[k : k + 2])) for k in range(0, len(fields), 2)]
    for half in halfway:
        out += from_lanes(matmul(stack_lanes(from_rows(half, n)), right), n)
    return out


def transform_back(grads, left, right):
    n = grads[0][0].shape[0]
    out = []
    halfway = [matmul(stack_lanes(grads[k : k + 2]), right) for k in range(0, len(grads), 2)]
    for half in halfway:
        result = matmul(left, stack_rows(from_lanes(half, n)))
        out += from_rows(result.astype(jnp.bfloat16).astype(jnp.float32), n)
    return out


def wave_kernel(
    scale, tile_rows, sizes,
    own_ref, live_ref, cross_ref, win_ref,
    probe_ref, cos_ref, sin_ref, fwd_ref, bwd_ref, measured_ref,
    probe_out_ref, grads_ref, *refs,
):
    *packed_refs, below_ref, packed, win, waves, cots, sems = refs
    capacity, planes, n, _ = win_ref.shape
    slices = planes // 2
    me = lax.axis_index(AXIS)
    live = live_ref[me]
    odd = me % 2 == 1

    def needs(slot):
        below, chunks = rows_below(own_ref, slot, me, tile_rows, n)
        return below, jnp.where(slot < live, chunks, 0)

    total = 0
    for slot in range(capacity):
        total += needs(slot)[1]

    def load(piece):
        part = pl.ds(piece * PIECE, PIECE)
        return pltpu.make_async_copy(cross_ref.at[part], below_ref.at[part], sems.at[piece])

    pieces = jnp.where(odd, (total + PIECE - 1) // PIECE, 0)

    @pl.loop(0, pieces)
    def _(piece):
        load(piece).start()

    @pl.loop(0, capacity)
    def _(slot):
        for p in range(planes):
            win[slot, p, pl.ds(0, n), :] = win_ref[slot, p].astype(jnp.float32)

    @pl.loop(0, pieces)
    def _(piece):
        load(piece).wait()

    def fill(slot, first):
        below, chunks = needs(slot)

        @pl.loop(0, chunks)
        def _(c):
            for p in range(planes):
                win[slot, p, pl.ds(n - below + c * CHUNK, CHUNK), :] = below_ref[
                    first + c, p
                ].astype(jnp.float32)

        return first + chunks

    lax.fori_loop(0, jnp.where(odd, live, 0), fill, 0)

    each = range(capacity)
    ahead, behind = fwd_ref[...], bwd_ref[...]

    def through(k, s):
        w_re, w_im = waves[k, s, 0], waves[k, s, 1]
        o_re, o_im = win[k, 2 * s, :n, :], win[k, 2 * s + 1, :n, :]
        return (w_re * o_re - w_im * o_im, w_re * o_im + w_im * o_re)

    def through_back(k, s):
        g_re, g_im = cots[k, 0], cots[k, 1]
        w_re, w_im = waves[k, s, 0], waves[k, s, 1]
        o_re, o_im = win[k, 2 * s, :n, :], win[k, 2 * s + 1, :n, :]
        d_re = g_re * w_re + g_im * w_im
        d_im = g_im * w_re - g_re * w_im
        win[k, 2 * s, :n, :] = d_re
        win[k, 2 * s + 1, :n, :] = d_im
        grads_ref[k, 2 * s] = d_re.astype(jnp.bfloat16)
        grads_ref[k, 2 * s + 1] = d_im.astype(jnp.bfloat16)
        return (g_re * o_re + g_im * o_im, g_im * o_re - g_re * o_im)

    def keep(ref, k, field):
        ref[0] = field[0]
        ref[1] = field[1]

    for k in each:
        keep(waves.at[k, 0], k, (probe_ref[0], probe_ref[1]))

    @pl.loop(0, slices - 1)
    def _(s):
        fields = transform([through(k, s) for k in each], ahead, behind)
        h_re, h_im = cos_ref[...], sin_ref[...]
        fields = [(a * h_re - b * h_im, a * h_im + b * h_re) for a, b in fields]
        fields = transform(fields, behind, ahead)
        for k in each:
            keep(waves.at[k, s + 1], k, fields[k])

    fields = transform([through(k, slices - 1) for k in each], ahead, behind)
    for k in each:
        f_re, f_im = fields[k]
        weight = jnp.where(k < live, 2.0, 0.0)
        target = measured_ref[k].astype(jnp.float32)
        inverse = lax.rsqrt(f_re * f_re + f_im * f_im + RIDGE)
        slope = weight * (1.0 - target * inverse)
        fields[k] = (slope * f_re, slope * f_im)
    fields = transform_back(fields, behind, ahead)
    for k in each:
        keep(cots.at[k], k, fields[k])

    @pl.loop(0, slices - 1)
    def _(step):
        s = slices - 1 - step
        fields = transform_back([through_back(k, s) for k in each], ahead, behind)
        h_re, h_im = cos_ref[...], sin_ref[...]
        fields = [(a * h_re + b * h_im, b * h_re - a * h_im) for a, b in fields]
        fields = transform_back(fields, behind, ahead)
        for k in each:
            keep(cots.at[k], k, fields[k])

    fields = [through_back(k, 0) for k in each]
    for part in range(2):
        sum_of = fields[0][part]
        for k in range(1, capacity):
            sum_of = sum_of + fields[k][part]
        probe_out_ref[part] = (sum_of * scale).astype(jnp.bfloat16)

    def hand_on(slot, first):
        below, chunks = needs(slot)

        @pl.when(chunks > 0)
        def _():
            for p in range(planes):
                win[slot, p, pl.ds(n, CHUNK), :] = jnp.zeros((CHUNK, LANES), jnp.float32)

        @pl.loop(0, chunks)
        def _(c):
            for p in range(planes):
                packed[first + c, p] = win[
                    slot, p, pl.ds(n - below + c * CHUNK, CHUNK), :
                ].astype(jnp.bfloat16)

        return first + chunks

    lax.fori_loop(0, live, hand_on, 0)
    level = level_of(total, sizes)
    for i, size in enumerate(sizes):
        target = (total > 0) & jnp.where(odd, level == i, size == sizes[-1])

        @pl.when(target)
        def _():
            store = pltpu.make_async_copy(packed.at[pl.ds(0, size)], packed_refs[i], sems.at[0])
            store.start()
            store.wait()


def run_waves(scale, tile_rows, own, live_counts, from_cross, win, probe, h_re, h_im, tables, measured):
    capacity, planes, n, _ = win.shape
    sizes = level_sizes(from_cross.shape[0])
    probe_part, grads, *packed = pl.pallas_call(
        functools.partial(wave_kernel, scale, tile_rows, sizes),
        out_shape=[
            jax.ShapeDtypeStruct(probe.shape, jnp.bfloat16),
            jax.ShapeDtypeStruct(win.shape, jnp.bfloat16),
        ]
        + [jax.ShapeDtypeStruct((size, planes, CHUNK, LANES), jnp.bfloat16) for size in sizes],
        in_specs=[SMEM] * 2 + [ANY] + [VMEM] * 7,
        out_specs=[VMEM] * 2 + [ANY] * len(sizes),
        scratch_shapes=[
            pltpu.VMEM(from_cross.shape, jnp.bfloat16),
            pltpu.VMEM(from_cross.shape, jnp.bfloat16),
            pltpu.VMEM((capacity, planes, n + CHUNK, LANES), jnp.float32),
            pltpu.VMEM((capacity, planes // 2, 2, n, n), jnp.float32),
            pltpu.VMEM((capacity, 2, n, n), jnp.float32),
            pltpu.SemaphoreType.DMA((sizes[-1] // PIECE,)),
        ],
        compiler_params=params(32),
        name="waves",
    )(own, live_counts, from_cross, win, probe, h_re, h_im, *tables, measured)
    return probe_part, grads, packed


def deposit_kernel(own_ref, live_ref, grads_ref, object_ref, top_ref, acc, sems):
    capacity, planes, n, _ = grads_ref.shape
    tile_rows = object_ref.shape[1]
    blocks = object_ref.shape[2] // LANES
    me = lax.axis_index(AXIS)

    @pl.loop(0, planes)
    def _(p):
        @pl.loop(0, blocks, unroll=2)
        def _(b):
            acc[p, b] = jnp.zeros(acc.shape[2:], jnp.float32)

    @pl.loop(0, live_ref[me])
    def _(slot):
        block, shift = place(own_ref, slot, blocks)
        rows = pl.ds(own_ref[0, slot] - me * tile_rows, n)
        table = selector(shift, True)

        @pl.loop(0, planes, unroll=2)
        def _(p):
            wide = matmul(grads_ref[slot, p], table)
            acc[p, block, rows, :] += wide[:, :LANES]
            acc[p, block + 1, rows, :] += wide[:, LANES:]

    def stores(b):
        rest = pl.ds(n, tile_rows - n)
        return (
            pltpu.make_async_copy(
                acc.at[:, b, rest, :],
                object_ref.at[:, rest, pl.ds(pl.multiple_of(b * LANES, LANES), LANES)],
                sems.at[b],
            ),
            pltpu.make_async_copy(
                acc.at[:, b, pl.ds(0, n), :], top_ref.at[:, b], sems.at[blocks + b]
            ),
        )

    @pl.loop(0, blocks)
    def _(b):
        for store in stores(b):
            store.start()

    @pl.loop(0, blocks)
    def _(b):
        for store in stores(b):
            store.wait()


def deposit(own, live_counts, grads, tile_rows, width):
    capacity, planes, n, _ = grads.shape
    blocks = width // LANES
    return pl.pallas_call(
        deposit_kernel,
        out_shape=(
            jax.ShapeDtypeStruct((planes, tile_rows, width), jnp.float32),
            jax.ShapeDtypeStruct((planes, blocks, n, LANES), jnp.float32),
        ),
        in_specs=[SMEM, SMEM, VMEM],
        out_specs=(pl.BlockSpec(memory_space=pltpu.HBM), ANY),
        scratch_shapes=[
            pltpu.VMEM((planes, blocks, tile_rows + n, LANES), jnp.float32),
            pltpu.SemaphoreType.DMA((2 * blocks,)),
        ],
        compiler_params=params(16),
        cost_estimate=pl.CostEstimate(flops=10**9, bytes_accessed=10**7, transcendentals=0),
        name="deposit_windows",
    )(own, live_counts, grads)


def finish_kernel(
    prev_ref, live_ref, object_in_ref, top_ref, pair_ref, cross_ref, object_ref, back, acc, sems
):
    planes, blocks, n, _ = acc.shape
    tile_rows = object_ref.shape[1]
    capacity = prev_ref.shape[1]
    first_put = pair_ref.shape[0] // PIECE
    me = lax.axis_index(AXIS)
    odd = me % 2 == 1
    before = jnp.maximum(me - 1, 0)
    live = jnp.where(me > 0, live_ref[before], 0)

    def needs(slot):
        _, chunks = rows_below(prev_ref, slot, before, tile_rows, n)
        return jnp.where(slot < live, chunks, 0)

    total = 0
    for slot in range(capacity):
        total += needs(slot)

    def load(source, piece):
        part = pl.ds(piece * PIECE, PIECE)
        return pltpu.make_async_copy(source.at[part], back.at[part], sems.at[piece])

    pieces = (total + PIECE - 1) // PIECE

    @pl.loop(0, pieces)
    def _(piece):
        pl.when(odd)(load(pair_ref, piece).start)
        pl.when(jnp.logical_not(odd))(load(cross_ref, piece).start)

    def fetch(b):
        return pltpu.make_async_copy(top_ref.at[:, b], acc.at[:, b], sems.at[first_put + b])

    def put(b):
        return pltpu.make_async_copy(
            acc.at[:, b],
            object_ref.at[:, pl.ds(0, n), pl.ds(pl.multiple_of(b * LANES, LANES), LANES)],
            sems.at[first_put + b],
        )

    @pl.loop(0, blocks)
    def _(b):
        fetch(b).start()

    @pl.loop(0, pieces)
    def _(piece):
        load(pair_ref, piece).wait()

    @pl.loop(0, blocks)
    def _(b):
        fetch(b).wait()

    def add(slot, first):
        chunks = needs(slot)

        @pl.when(chunks > 0)
        def _():
            block, shift = place(prev_ref, slot, blocks)
            table = selector(shift, True)

            @pl.loop(0, planes, unroll=2)
            def _(p):
                parts = []
                for c in range(n // CHUNK):
                    part = back[first + c, p]
                    parts.append(jnp.where(c < chunks, part, jnp.zeros_like(part)))
                wide = matmul(jnp.concatenate(parts, 0), table)
                acc[p, block] += wide[:, :LANES]
                acc[p, block + 1] += wide[:, LANES:]

        return first + chunks

    lax.fori_loop(0, live, add, 0)

    @pl.loop(0, blocks)
    def _(b):
        put(b).start()

    @pl.loop(0, blocks)
    def _(b):
        put(b).wait()


def finish(prev, live_counts, grad, top, from_pair, from_cross):
    planes, blocks, n, _ = top.shape
    hbm = pl.BlockSpec(memory_space=pltpu.HBM)
    chunks = from_pair.shape[0]
    return pl.pallas_call(
        finish_kernel,
        out_shape=jax.ShapeDtypeStruct(grad.shape, grad.dtype),
        in_specs=[SMEM, SMEM, hbm, ANY, ANY, ANY],
        out_specs=hbm,
        input_output_aliases={2: 0},
        scratch_shapes=[
            pltpu.VMEM((chunks + n // CHUNK,) + from_pair.shape[1:], jnp.bfloat16),
            pltpu.VMEM(top.shape, jnp.float32),
            pltpu.SemaphoreType.DMA((chunks // PIECE + 1 + blocks,)),
        ],
        compiler_params=params(12),
        name="add_from_before",
    )(prev, live_counts, grad, top, from_pair, from_cross)


def local(transmission, probe_wavefield, phase_shift, offsets, live_counts, measured):
    slices, parts, tile_rows, width = transmission.shape
    n = probe_wavefield.shape[-1]
    capacity = offsets.shape[1]
    devices = lax.axis_size(AXIS)
    tile = transmission.reshape(slices * parts, tile_rows, width)
    prev = lax.ppermute(offsets, AXIS, [(i, i + 1) for i in range(devices - 1)])
    rim = within_pair(copied(tile, (slices * parts, n, width), n), False)
    phase = (jnp.cos(phase_shift), jnp.sin(phase_shift))
    level, packed = pack(offsets, prev, live_counts, tile, n, phase)
    from_cross, win = between_pairs_upto(
        level, packed, False, cut, (offsets, live_counts, tile, rim)
    )
    scale = 1.0 / math.sqrt(capacity * devices)
    probe_part, grads, packed = run_waves(
        scale, tile_rows, offsets, live_counts, from_cross, win,
        probe_wavefield, *phase, dft_tables(n), measured,
    )
    rounds = exchange_rounds(devices)
    back_pair = within_pair(packed[-1], True)
    terms = exchange(probe_part, rounds[0])
    back_cross, (grad, top) = between_pairs_upto(
        level, packed, True,
        lambda own, live, grads: deposit(own, live, grads, tile_rows, width),
        (offsets, live_counts, grads),
    )
    for i, steps in enumerate(rounds[1:]):
        terms = exchange(summed(terms, jnp.bfloat16, (top,) if i == 0 else ()), steps)
    probe_grad = summed(terms, jnp.float32)
    grad = finish(prev, live_counts, grad, top, back_pair, back_cross)
    return (grad.reshape(slices, parts, tile_rows, width), probe_grad)


def solution(mesh):
    in_specs = (
        P(None, None, ("groups", "ty"), None),
        P("groups", None, None),
        P(),
        P(None, ("groups", "ty")),
        P("groups"),
        P(("groups", "ty"), None, None),
    )
    out_specs = (P(None, None, ("groups", "ty"), None), P("groups", None, None))
    return jax.shard_map(local, mesh=mesh, in_specs=in_specs, out_specs=out_specs, check_vma=False)
```

```python
import functools
import math

import jax
import jax.numpy as jnp
import numpy as np
from jax import lax
from jax.experimental import pallas as pl
from jax.experimental.pallas import tpu as pltpu
from jax.sharding import PartitionSpec as P

RIDGE = 0.25
LANES = 128
CHUNK = 16
PIECE = 8
AXIS = "ty"

ANY = pl.BlockSpec(memory_space=pl.ANY)
VMEM = pl.BlockSpec(memory_space=pltpu.VMEM)
SMEM = pl.BlockSpec(memory_space=pltpu.SMEM)


def params(mib):
    return pltpu.CompilerParams(vmem_limit_bytes=mib * 2**20)


def matmul(a, b):
    return jnp.dot(a, b, preferred_element_type=jnp.float32)


def within_pair(block, up):
    devices = lax.axis_size(AXIS)
    pairs = [(i + 1, i) for i in range(0, devices - 1, 2)]
    if up:
        pairs = [(b, a) for a, b in pairs]
    return lax.ppermute(block, AXIS, pairs)


def between_pairs(block, up):
    devices = lax.axis_size(AXIS)
    pairs = [(i + 1, i) for i in range(1, devices - 1, 2)]
    if up:
        pairs = [(b, a) for a, b in pairs]
    return lax.ppermute(block, AXIS, pairs)


def level_sizes(chunks):
    return (3 * chunks // 8, chunks // 2, chunks)


def level_of(total, sizes):
    level = 0
    for size in sizes[:-1]:
        level += jnp.where(total > size, 1, 0)
    return level


def place_kernel(source_ref, target_ref, sem):
    copy = pltpu.make_async_copy(source_ref, target_ref.at[pl.ds(0, source_ref.shape[0])], sem)
    copy.start()
    copy.wait()


def placed(block, shape):
    return pl.pallas_call(
        place_kernel,
        out_shape=jax.ShapeDtypeStruct(shape, block.dtype),
        in_specs=[ANY],
        out_specs=ANY,
        scratch_shapes=[pltpu.SemaphoreType.DMA],
        compiler_params=params(2),
        name="place_chunks",
    )(block)


def between_pairs_upto(level, packed, up, beside, operands):
    full = packed[-1].shape

    def branch(i):
        def run(packed, *operands):
            got = between_pairs(packed[i], up)
            other = beside(*operands)
            if got.shape != full:
                got = placed(got, full)
            return got, other

        return run

    return lax.switch(level, [branch(i) for i in range(len(packed))], packed, *operands)


def sum_kernel(count, *refs):
    terms = [ref[...].astype(jnp.float32) for ref in refs[:count]]
    if count == 2:
        total = terms[0] + terms[1]
    else:
        total = (terms[0] + terms[1]) + (terms[2] + terms[3])
    out_ref = refs[-1]
    out_ref[...] = total.astype(out_ref.dtype)


def exchange(block, steps):
    devices = lax.axis_size(AXIS)
    return [block] + [lax.ppermute(block, AXIS, [(i, i ^ s) for i in range(devices)]) for s in steps]


def summed(terms, dtype, after=()):
    return pl.pallas_call(
        functools.partial(sum_kernel, len(terms)),
        out_shape=jax.ShapeDtypeStruct(terms[0].shape, dtype),
        in_specs=[VMEM] * len(terms) + [ANY] * len(after),
        out_specs=VMEM,
        compiler_params=params(4),
        name="sum_partners",
    )(*terms, *after)


def exchange_rounds(devices):
    rounds = []
    step = 1
    while step < devices:
        if step * 2 < devices:
            rounds.append((step, 2 * step, 3 * step))
        else:
            rounds.append((step,))
        step *= 4
    return rounds[::-1]


def place(offsets_ref, slot, blocks):
    col = offsets_ref[1, slot]
    block = jnp.minimum(col // LANES, blocks - 2)
    return block, col - block * LANES


def rows_below(offsets_ref, slot, owner, tile_rows, n):
    below = jnp.maximum(offsets_ref[0, slot] - owner * tile_rows + n - tile_rows, 0)
    return below, (below + CHUNK - 1) // CHUNK


def selector(shift, transposed):
    shape = (LANES, 2 * LANES) if transposed else (2 * LANES, LANES)
    wide = lax.broadcasted_iota(jnp.int32, shape, 1 if transposed else 0)
    narrow = lax.broadcasted_iota(jnp.int32, shape, 0 if transposed else 1)
    return jnp.where(wide == narrow + shift, 1.0, 0.0).astype(jnp.bfloat16)


def pack_kernel(sizes, own_ref, prev_ref, live_ref, tile_ref, *refs):
    level_ref, *packed_refs, buf, packed, sems = refs[2:]
    planes, tile_rows, width = tile_ref.shape
    n = buf.shape[2]
    blocks = width // LANES
    capacity = own_ref.shape[1]
    me = lax.axis_index(AXIS)
    odd = me % 2 == 1
    before = jnp.maximum(me - 1, 0)
    live_before = jnp.where((me > 0) & jnp.logical_not(odd), live_ref[before], 0)
    live_own = live_ref[me]

    def needs(slot):
        below, chunks = rows_below(prev_ref, slot, before, tile_rows, n)
        return jnp.where(slot < live_before, chunks, 0)

    def load(slot):
        block, _ = place(prev_ref, slot, blocks)
        cols = pl.ds(pl.multiple_of(block * LANES, LANES), 2 * LANES)
        return pltpu.make_async_copy(
            tile_ref.at[:, pl.ds(0, n), cols], buf.at[slot], sems.at[slot]
        )

    @pl.loop(0, live_before)
    def _(slot):
        pl.when(needs(slot) > 0)(load(slot).start)

    total_own = 0
    for slot in range(capacity):
        _, chunks = rows_below(own_ref, slot, me, tile_rows, n)
        total_own += jnp.where(slot < live_own, chunks, 0)

    def pack(slot, first):
        chunks = needs(slot)

        @pl.when(chunks > 0)
        def _():
            load(slot).wait()
            _, shift = place(prev_ref, slot, blocks)
            table = selector(shift, False)
            for p in range(planes):
                rows = matmul(buf[slot, p], table).astype(jnp.bfloat16)
                for c in range(n // CHUNK):
                    packed[first + c, p] = rows[c * CHUNK : (c + 1) * CHUNK]

        return first + chunks

    total_before = lax.fori_loop(0, live_before, pack, 0)
    level = level_of(jnp.where(odd, total_own, total_before), sizes)
    level_ref[0] = level
    for i, size in enumerate(sizes):
        @pl.when((level == i) & (total_before > 0))
        def _():
            store = pltpu.make_async_copy(
                packed.at[pl.ds(0, size)], packed_refs[i], sems.at[capacity]
            )
            store.start()
            store.wait()


def pack(own, prev, live_counts, tile, n, after):
    planes = tile.shape[0]
    capacity = own.shape[1]
    sizes = level_sizes(capacity * (n // CHUNK))
    level, *packed = pl.pallas_call(
        functools.partial(pack_kernel, sizes),
        out_shape=[jax.ShapeDtypeStruct((1,), jnp.int32)]
        + [jax.ShapeDtypeStruct((size, planes, CHUNK, LANES), jnp.bfloat16) for size in sizes],
        in_specs=[SMEM, SMEM, SMEM, ANY] + [ANY] * len(after),
        out_specs=[SMEM] + [ANY] * len(sizes),
        scratch_shapes=[
            pltpu.VMEM((capacity, planes, n, 2 * LANES), jnp.bfloat16),
            pltpu.VMEM((sizes[-1] + n // CHUNK, planes, CHUNK, LANES), jnp.bfloat16),
            pltpu.SemaphoreType.DMA((capacity + 1,)),
        ],
        compiler_params=params(12),
        name="pack_rows",
    )(own, prev, live_counts, tile, *after)
    return level[0], packed


def cut_kernel(own_ref, live_ref, tile_ref, win_ref, buf, slab, sems):
    planes, tile_rows, width = tile_ref.shape
    n = win_ref.shape[2]
    blocks = width // LANES
    capacity = own_ref.shape[1]
    tall = n + CHUNK
    me = lax.axis_index(AXIS)
    live = live_ref[me]

    def top(slot):
        row = own_ref[0, slot] - me * tile_rows
        base = jnp.minimum(row // CHUNK * CHUNK, tile_rows - tall)
        return pl.multiple_of(base, CHUNK), row - base

    def load(slot):
        block, _ = place(own_ref, slot, blocks)
        cols = pl.ds(pl.multiple_of(block * LANES, LANES), 2 * LANES)
        base, _ = top(slot)
        return pltpu.make_async_copy(
            tile_ref.at[:, pl.ds(base, tall), cols], buf.at[slot], sems.at[slot]
        )

    @pl.loop(0, live)
    def _(slot):
        load(slot).start()

    @pl.loop(0, capacity)
    def _(slot):
        @pl.when(slot < live)
        def _():
            load(slot).wait()
            _, shift = place(own_ref, slot, blocks)
            _, skip = top(slot)
            table = selector(shift, False)
            for p in range(planes):
                slab[p, pl.ds(0, tall), :] = matmul(buf[slot, p], table)
            for p in range(planes):
                win_ref[slot, p] = slab[p, pl.ds(skip, n), :].astype(jnp.bfloat16)

        @pl.when(slot >= live)
        def _():
            @pl.loop(0, planes)
            def _(p):
                win_ref[slot, p] = jnp.zeros(win_ref.shape[2:], jnp.bfloat16)


def cut(own, live_counts, tile, n):
    planes = tile.shape[0]
    capacity = own.shape[1]
    tall = n + CHUNK
    return pl.pallas_call(
        cut_kernel,
        out_shape=jax.ShapeDtypeStruct((capacity, planes, n, LANES), jnp.bfloat16),
        in_specs=[SMEM, SMEM, ANY],
        out_specs=VMEM,
        scratch_shapes=[
            pltpu.VMEM((capacity, planes, tall, 2 * LANES), jnp.bfloat16),
            pltpu.VMEM((planes, tall + n, LANES), jnp.float32),
            pltpu.SemaphoreType.DMA((capacity,)),
        ],
        compiler_params=params(16),
        cost_estimate=pl.CostEstimate(flops=10**9, bytes_accessed=10**7, transcendentals=0),
        name="cut_windows",
    )(own, live_counts, tile)


def dft_tables(n):
    positions = np.arange(n)
    product = positions[:, None] * positions[None, :] % n
    angles = 2.0 * math.pi / n * product
    real = np.cos(angles) / math.sqrt(n)
    imag = -np.sin(angles) / math.sqrt(n)
    left = np.block([[real, -imag], [imag, real]])
    return (jnp.asarray(left, jnp.bfloat16), jnp.asarray(left.T, jnp.bfloat16))


def stack_rows(fields):
    return jnp.concatenate(
        [jnp.concatenate([re, im], 0).astype(jnp.bfloat16) for re, im in fields], 1
    )


def stack_lanes(fields):
    return jnp.concatenate(
        [jnp.concatenate([re, im], 1).astype(jnp.bfloat16) for re, im in fields], 0
    )


def from_rows(block, n):
    return [(block[:n, k * n : (k + 1) * n], block[n:, k * n : (k + 1) * n]) for k in range(2)]


def from_lanes(block, n):
    return [(block[k * n : (k + 1) * n, :n], block[k * n : (k + 1) * n, n:]) for k in range(2)]


def transform(fields, left, right):
    n = fields[0][0].shape[0]
    out = []
    halfway = [matmul(left, stack_rows(fields[k : k + 2])) for k in range(0, len(fields), 2)]
    for half in halfway:
        out += from_lanes(matmul(stack_lanes(from_rows(half, n)), right), n)
    return out


def transform_back(grads, left, right):
    n = grads[0][0].shape[0]
    out = []
    halfway = [matmul(stack_lanes(grads[k : k + 2]), right) for k in range(0, len(grads), 2)]
    for half in halfway:
        result = matmul(left, stack_rows(from_lanes(half, n)))
        out += from_rows(result.astype(jnp.bfloat16).astype(jnp.float32), n)
    return out


def wave_kernel(
    scale, tile_rows, sizes,
    own_ref, live_ref, next_ref, cross_ref, win_ref,
    probe_ref, cos_ref, sin_ref, fwd_ref, bwd_ref, measured_ref,
    probe_out_ref, grads_ref, *refs,
):
    *packed_refs, below_ref, rims, packed, win, waves, cots, sems = refs
    blocks = next_ref.shape[2] // LANES
    capacity, planes, n, _ = win_ref.shape
    slices = planes // 2
    me = lax.axis_index(AXIS)
    live = live_ref[me]
    odd = me % 2 == 1

    def needs(slot):
        below, chunks = rows_below(own_ref, slot, me, tile_rows, n)
        return below, jnp.where(slot < live, chunks, 0)

    total = 0
    for slot in range(capacity):
        total += needs(slot)[1]

    def load(piece):
        part = pl.ds(piece * PIECE, PIECE)
        return pltpu.make_async_copy(cross_ref.at[part], below_ref.at[part], sems.at[piece])

    def load_rim(slot):
        block, _ = place(own_ref, slot, blocks)
        cols = pl.ds(pl.multiple_of(block * LANES, LANES), 2 * LANES)
        return pltpu.make_async_copy(
            next_ref.at[:, pl.ds(0, n), cols], rims.at[slot], sems.at[slot]
        )

    pieces = jnp.where(odd, (total + PIECE - 1) // PIECE, 0)

    @pl.loop(0, pieces)
    def _(piece):
        load(piece).start()

    @pl.when(jnp.logical_not(odd))
    def _():
        @pl.loop(0, live)
        def _(slot):
            pl.when(needs(slot)[1] > 0)(load_rim(slot).start)

    @pl.loop(0, capacity)
    def _(slot):
        for p in range(planes):
            win[slot, p, pl.ds(0, n), :] = win_ref[slot, p].astype(jnp.float32)

    @pl.loop(0, pieces)
    def _(piece):
        load(piece).wait()

    def fill(slot, first):
        below, chunks = needs(slot)

        @pl.when((chunks > 0) & odd)
        def _():
            @pl.loop(0, planes, unroll=2)
            def _(p):
                for c in range(n // CHUNK):
                    win[slot, p, pl.ds(n - below + c * CHUNK, CHUNK), :] = below_ref[
                        first + c, p
                    ].astype(jnp.float32)

        @pl.when((chunks > 0) & jnp.logical_not(odd))
        def _():
            load_rim(slot).wait()
            _, shift = place(own_ref, slot, blocks)
            table = selector(shift, False)
            for p in range(planes):
                win[slot, p, pl.ds(n - below, n), :] = matmul(rims[slot, p], table)

        return first + chunks

    lax.fori_loop(0, live, fill, 0)

    each = range(capacity)
    ahead, behind = fwd_ref[...], bwd_ref[...]

    def through(k, s):
        w_re, w_im = waves[k, s, 0], waves[k, s, 1]
        o_re, o_im = win[k, 2 * s, :n, :], win[k, 2 * s + 1, :n, :]
        return (w_re * o_re - w_im * o_im, w_re * o_im + w_im * o_re)

    def through_back(k, s):
        g_re, g_im = cots[k, 0], cots[k, 1]
        w_re, w_im = waves[k, s, 0], waves[k, s, 1]
        o_re, o_im = win[k, 2 * s, :n, :], win[k, 2 * s + 1, :n, :]
        d_re = g_re * w_re + g_im * w_im
        d_im = g_im * w_re - g_re * w_im
        win[k, 2 * s, :n, :] = d_re
        win[k, 2 * s + 1, :n, :] = d_im
        grads_ref[k, 2 * s] = d_re.astype(jnp.bfloat16)
        grads_ref[k, 2 * s + 1] = d_im.astype(jnp.bfloat16)
        return (g_re * o_re + g_im * o_im, g_im * o_re - g_re * o_im)

    def keep(ref, k, field):
        ref[0] = field[0]
        ref[1] = field[1]

    for k in each:
        keep(waves.at[k, 0], k, (probe_ref[0], probe_ref[1]))

    @pl.loop(0, slices - 1)
    def _(s):
        fields = transform([through(k, s) for k in each], ahead, behind)
        h_re, h_im = cos_ref[...], sin_ref[...]
        fields = [(a * h_re - b * h_im, a * h_im + b * h_re) for a, b in fields]
        fields = transform(fields, behind, ahead)
        for k in each:
            keep(waves.at[k, s + 1], k, fields[k])

    fields = transform([through(k, slices - 1) for k in each], ahead, behind)
    for k in each:
        f_re, f_im = fields[k]
        weight = jnp.where(k < live, 2.0, 0.0)
        target = measured_ref[k].astype(jnp.float32)
        inverse = lax.rsqrt(f_re * f_re + f_im * f_im + RIDGE)
        slope = weight * (1.0 - target * inverse)
        fields[k] = (slope * f_re, slope * f_im)
    fields = transform_back(fields, behind, ahead)
    for k in each:
        keep(cots.at[k], k, fields[k])

    @pl.loop(0, slices - 1)
    def _(step):
        s = slices - 1 - step
        fields = transform_back([through_back(k, s) for k in each], ahead, behind)
        h_re, h_im = cos_ref[...], sin_ref[...]
        fields = [(a * h_re + b * h_im, b * h_re - a * h_im) for a, b in fields]
        fields = transform_back(fields, behind, ahead)
        for k in each:
            keep(cots.at[k], k, fields[k])

    fields = [through_back(k, 0) for k in each]
    for part in range(2):
        sum_of = fields[0][part]
        for k in range(1, capacity):
            sum_of = sum_of + fields[k][part]
        probe_out_ref[part] = (sum_of * scale).astype(jnp.bfloat16)

    def hand_on(slot, first):
        below, chunks = needs(slot)

        @pl.when(chunks > 0)
        def _():
            for p in range(planes):
                win[slot, p, pl.ds(n, CHUNK), :] = jnp.zeros((CHUNK, LANES), jnp.float32)

            @pl.loop(0, planes, unroll=2)
            def _(p):
                for c in range(n // CHUNK):
                    packed[first + c, p] = win[
                        slot, p, pl.ds(n - below + c * CHUNK, CHUNK), :
                    ].astype(jnp.bfloat16)

        return first + chunks

    lax.fori_loop(0, live, hand_on, 0)
    level = level_of(total, sizes)
    for i, size in enumerate(sizes):
        target = (total > 0) & jnp.where(odd, level == i, size == sizes[-1])

        @pl.when(target)
        def _():
            store = pltpu.make_async_copy(packed.at[pl.ds(0, size)], packed_refs[i], sems.at[0])
            store.start()
            store.wait()


def run_waves(scale, tile_rows, own, live_counts, next_tile, from_cross, win, probe, h_re, h_im, tables, measured):
    capacity, planes, n, _ = win.shape
    sizes = level_sizes(from_cross.shape[0])
    padded = (sizes[-1] + n // CHUNK, planes, CHUNK, LANES)
    probe_part, grads, *packed = pl.pallas_call(
        functools.partial(wave_kernel, scale, tile_rows, sizes),
        out_shape=[
            jax.ShapeDtypeStruct(probe.shape, jnp.bfloat16),
            jax.ShapeDtypeStruct(win.shape, jnp.bfloat16),
        ]
        + [jax.ShapeDtypeStruct((size, planes, CHUNK, LANES), jnp.bfloat16) for size in sizes],
        in_specs=[SMEM] * 2 + [ANY] * 2 + [VMEM] * 7,
        out_specs=[VMEM] * 2 + [ANY] * len(sizes),
        scratch_shapes=[
            pltpu.VMEM(padded, jnp.bfloat16),
            pltpu.VMEM((capacity, planes, n, 2 * LANES), jnp.bfloat16),
            pltpu.VMEM(padded, jnp.bfloat16),
            pltpu.VMEM((capacity, planes, 2 * n, LANES), jnp.float32),
            pltpu.VMEM((capacity, planes // 2, 2, n, n), jnp.float32),
            pltpu.VMEM((capacity, 2, n, n), jnp.float32),
            pltpu.SemaphoreType.DMA((max(capacity, sizes[-1] // PIECE),)),
        ],
        compiler_params=params(36),
        name="waves",
    )(own, live_counts, next_tile, from_cross, win, probe, h_re, h_im, *tables, measured)
    return probe_part, grads, packed


def deposit_kernel(own_ref, live_ref, grads_ref, object_ref, top_ref, acc, sems):
    capacity, planes, n, _ = grads_ref.shape
    tile_rows = object_ref.shape[1]
    blocks = object_ref.shape[2] // LANES
    me = lax.axis_index(AXIS)

    @pl.loop(0, planes)
    def _(p):
        @pl.loop(0, blocks, unroll=2)
        def _(b):
            acc[p, b] = jnp.zeros(acc.shape[2:], jnp.float32)

    @pl.loop(0, live_ref[me])
    def _(slot):
        block, shift = place(own_ref, slot, blocks)
        rows = pl.ds(own_ref[0, slot] - me * tile_rows, n)
        table = selector(shift, True)

        for p in range(planes):
            wide = matmul(grads_ref[slot, p], table)
            acc[p, block, rows, :] += wide[:, :LANES]
            acc[p, block + 1, rows, :] += wide[:, LANES:]

    def stores(b):
        rest = pl.ds(n, tile_rows - n)
        return (
            pltpu.make_async_copy(
                acc.at[:, b, rest, :],
                object_ref.at[:, rest, pl.ds(pl.multiple_of(b * LANES, LANES), LANES)],
                sems.at[b],
            ),
            pltpu.make_async_copy(
                acc.at[:, b, pl.ds(0, n), :], top_ref.at[:, b], sems.at[blocks + b]
            ),
        )

    @pl.loop(0, blocks)
    def _(b):
        for store in stores(b):
            store.start()

    @pl.loop(0, blocks)
    def _(b):
        for store in stores(b):
            store.wait()


def deposit(own, live_counts, grads, tile_rows, width):
    capacity, planes, n, _ = grads.shape
    blocks = width // LANES
    return pl.pallas_call(
        deposit_kernel,
        out_shape=(
            jax.ShapeDtypeStruct((planes, tile_rows, width), jnp.float32),
            jax.ShapeDtypeStruct((planes, blocks, n, LANES), jnp.float32),
        ),
        in_specs=[SMEM, SMEM, VMEM],
        out_specs=(pl.BlockSpec(memory_space=pltpu.HBM), ANY),
        scratch_shapes=[
            pltpu.VMEM((planes, blocks, tile_rows + n, LANES), jnp.float32),
            pltpu.SemaphoreType.DMA((2 * blocks,)),
        ],
        compiler_params=params(54),
        cost_estimate=pl.CostEstimate(flops=10**9, bytes_accessed=10**7, transcendentals=0),
        name="deposit_windows",
    )(own, live_counts, grads)


def finish_kernel(
    prev_ref, live_ref, object_in_ref, top_ref, pair_ref, cross_ref, object_ref, back, acc, sems
):
    planes, blocks, n, _ = acc.shape
    tile_rows = object_ref.shape[1]
    capacity = prev_ref.shape[1]
    first_put = pair_ref.shape[0] // PIECE
    me = lax.axis_index(AXIS)
    odd = me % 2 == 1
    before = jnp.maximum(me - 1, 0)
    live = jnp.where(me > 0, live_ref[before], 0)

    def needs(slot):
        _, chunks = rows_below(prev_ref, slot, before, tile_rows, n)
        return jnp.where(slot < live, chunks, 0)

    total = 0
    for slot in range(capacity):
        total += needs(slot)

    def load(source, piece):
        part = pl.ds(piece * PIECE, PIECE)
        return pltpu.make_async_copy(source.at[part], back.at[part], sems.at[piece])

    pieces = (total + PIECE - 1) // PIECE

    @pl.loop(0, pieces)
    def _(piece):
        pl.when(odd)(load(pair_ref, piece).start)
        pl.when(jnp.logical_not(odd))(load(cross_ref, piece).start)

    def fetch(b):
        return pltpu.make_async_copy(top_ref.at[:, b], acc.at[:, b], sems.at[first_put + b])

    def put(b):
        return pltpu.make_async_copy(
            acc.at[:, b],
            object_ref.at[:, pl.ds(0, n), pl.ds(pl.multiple_of(b * LANES, LANES), LANES)],
            sems.at[first_put + b],
        )

    @pl.loop(0, blocks)
    def _(b):
        fetch(b).start()

    @pl.loop(0, pieces)
    def _(piece):
        load(pair_ref, piece).wait()

    @pl.loop(0, blocks)
    def _(b):
        fetch(b).wait()

    def add(slot, first):
        chunks = needs(slot)

        @pl.when(chunks > 0)
        def _():
            block, shift = place(prev_ref, slot, blocks)
            table = selector(shift, True)

            for p in range(planes):
                parts = []
                for c in range(n // CHUNK):
                    part = back[first + c, p]
                    parts.append(jnp.where(c < chunks, part, jnp.zeros_like(part)))
                wide = matmul(jnp.concatenate(parts, 0), table)
                acc[p, block] += wide[:, :LANES]
                acc[p, block + 1] += wide[:, LANES:]

        return first + chunks

    lax.fori_loop(0, live, add, 0)

    @pl.loop(0, blocks)
    def _(b):
        put(b).start()

    @pl.loop(0, blocks)
    def _(b):
        put(b).wait()


def finish(prev, live_counts, grad, top, from_pair, from_cross):
    planes, blocks, n, _ = top.shape
    hbm = pl.BlockSpec(memory_space=pltpu.HBM)
    chunks = from_pair.shape[0]
    return pl.pallas_call(
        finish_kernel,
        out_shape=jax.ShapeDtypeStruct(grad.shape, grad.dtype),
        in_specs=[SMEM, SMEM, hbm, ANY, ANY, ANY],
        out_specs=hbm,
        input_output_aliases={2: 0},
        scratch_shapes=[
            pltpu.VMEM((chunks + n // CHUNK,) + from_pair.shape[1:], jnp.bfloat16),
            pltpu.VMEM(top.shape, jnp.float32),
            pltpu.SemaphoreType.DMA((chunks // PIECE + 1 + blocks,)),
        ],
        compiler_params=params(50),
        cost_estimate=pl.CostEstimate(flops=10**9, bytes_accessed=2 * 10**7, transcendentals=0),
        name="add_from_before",
    )(prev, live_counts, grad, top, from_pair, from_cross)


def local(transmission, probe_wavefield, phase_shift, offsets, live_counts, measured):
    slices, parts, tile_rows, width = transmission.shape
    n = probe_wavefield.shape[-1]
    capacity = offsets.shape[1]
    devices = lax.axis_size(AXIS)
    tile = transmission.reshape(slices * parts, tile_rows, width)
    prev = lax.ppermute(offsets, AXIS, [(i, i + 1) for i in range(devices - 1)])
    next_tile = within_pair(tile, False)
    phase = (jnp.cos(phase_shift), jnp.sin(phase_shift))
    level, packed = pack(offsets, prev, live_counts, tile, n, phase)
    from_cross, win = between_pairs_upto(
        level, packed, False,
        lambda own, live, tile: cut(own, live, tile, n),
        (offsets, live_counts, tile),
    )
    scale = 1.0 / math.sqrt(capacity * devices)
    probe_part, grads, packed = run_waves(
        scale, tile_rows, offsets, live_counts, next_tile, from_cross, win,
        probe_wavefield, *phase, dft_tables(n), measured,
    )
    rounds = exchange_rounds(devices)
    back_pair = within_pair(packed[-1], True)
    terms = exchange(probe_part, rounds[0])
    back_cross, (grad, top) = between_pairs_upto(
        level, packed, True,
        lambda own, live, grads: deposit(own, live, grads, tile_rows, width),
        (offsets, live_counts, grads),
    )
    for i, steps in enumerate(rounds[1:]):
        terms = exchange(summed(terms, jnp.bfloat16, (top,) if i == 0 else ()), steps)
    grad = finish(prev, live_counts, grad, top, back_pair, back_cross)
    probe_grad = summed(terms, jnp.float32, (grad,))
    return (grad.reshape(slices, parts, tile_rows, width), probe_grad)


def solution(mesh):
    in_specs = (
        P(None, None, ("groups", "ty"), None),
        P("groups", None, None),
        P(),
        P(None, ("groups", "ty")),
        P("groups"),
        P(("groups", "ty"), None, None),
    )
    out_specs = (P(None, None, ("groups", "ty"), None), P("groups", None, None))
    return jax.shard_map(local, mesh=mesh, in_specs=in_specs, out_specs=out_specs, check_vma=False)
```

```python
import functools
import math

import jax
import jax.numpy as jnp
import numpy as np
from jax import lax
from jax.experimental import pallas as pl
from jax.experimental.pallas import tpu as pltpu
from jax.sharding import PartitionSpec as P

RIDGE = 0.25
LANES = 128
CHUNK = 16
PIECE = 8
ROW_PAD = 8
AXIS = "ty"

ANY = pl.BlockSpec(memory_space=pl.ANY)
VMEM = pl.BlockSpec(memory_space=pltpu.VMEM)
SMEM = pl.BlockSpec(memory_space=pltpu.SMEM)


def params(mib):
    return pltpu.CompilerParams(vmem_limit_bytes=mib * 2**20)


def matmul(a, b):
    return jnp.dot(a, b, preferred_element_type=jnp.float32)


def within_pair(block, up):
    devices = lax.axis_size(AXIS)
    pairs = [(i + 1, i) for i in range(0, devices - 1, 2)]
    if up:
        pairs = [(b, a) for a, b in pairs]
    return lax.ppermute(block, AXIS, pairs)


def between_pairs(block, up):
    devices = lax.axis_size(AXIS)
    pairs = [(i + 1, i) for i in range(1, devices - 1, 2)]
    if up:
        pairs = [(b, a) for a, b in pairs]
    return lax.ppermute(block, AXIS, pairs)


def level_sizes(chunks):
    return (3 * chunks // 8, chunks // 2, 5 * chunks // 8, chunks)


def level_of(total, sizes):
    level = 0
    for size in sizes[:-1]:
        level += jnp.where(total > size, 1, 0)
    return level


def place_kernel(source_ref, target_ref, sem):
    copy = pltpu.make_async_copy(source_ref, target_ref.at[pl.ds(0, source_ref.shape[0])], sem)
    copy.start()
    copy.wait()


def placed(block, shape):
    return pl.pallas_call(
        place_kernel,
        out_shape=jax.ShapeDtypeStruct(shape, block.dtype),
        in_specs=[ANY],
        out_specs=ANY,
        scratch_shapes=[pltpu.SemaphoreType.DMA],
        compiler_params=params(2),
        name="place_chunks",
    )(block)


def between_pairs_upto(level, packed, up, beside, operands):
    full = packed[-1].shape

    def branch(i):
        def run(packed, *operands):
            got = between_pairs(packed[i], up)
            other = beside(*operands)
            if got.shape != full:
                got = placed(got, full)
            return got, other

        return run

    return lax.switch(level, [branch(i) for i in range(len(packed))], packed, *operands)


def sum_kernel(share_ref, after_ref, out_ref):
    total = jnp.sum(share_ref[...].astype(jnp.float32), 0)
    out_ref[...] = jnp.broadcast_to(total.astype(out_ref.dtype)[None], out_ref.shape)


def scattered(block):
    devices = lax.axis_size(AXIS)
    shares = block.reshape(devices, -1, LANES)
    return lax.all_to_all(shares, AXIS, 0, 0)


def summed_shares(shares, after):
    return pl.pallas_call(
        sum_kernel,
        out_shape=jax.ShapeDtypeStruct(shares.shape, shares.dtype),
        in_specs=[VMEM, ANY],
        out_specs=VMEM,
        compiler_params=params(4),
        name="sum_shares",
    )(shares, after)


def place(offsets_ref, slot, blocks):
    col = offsets_ref[1, slot]
    block = jnp.minimum(col // LANES, blocks - 2)
    return block, col - block * LANES


def rows_below(offsets_ref, slot, owner, tile_rows, n):
    below = jnp.maximum(offsets_ref[0, slot] - owner * tile_rows + n - tile_rows, 0)
    return below, (below + CHUNK - 1) // CHUNK


def window_lanes(left, right, shift):
    lane = lax.broadcasted_iota(jnp.int32, left.shape, 1)
    back = lax.rem(LANES - shift, LANES)
    left = pltpu.roll(left.astype(jnp.float32), back, 1)
    right = pltpu.roll(right.astype(jnp.float32), back, 1)
    return jnp.where(lane < LANES - shift, left, right)


def selector(shift, transposed):
    shape = (LANES, 2 * LANES) if transposed else (2 * LANES, LANES)
    wide = lax.broadcasted_iota(jnp.int32, shape, 1 if transposed else 0)
    narrow = lax.broadcasted_iota(jnp.int32, shape, 0 if transposed else 1)
    return jnp.where(wide == narrow + shift, 1.0, 0.0).astype(jnp.bfloat16)


def pack_kernel(sizes, own_ref, prev_ref, live_ref, tile_ref, *refs):
    level_ref, *packed_refs, buf, packed, sems = refs
    planes, tile_rows, width = tile_ref.shape
    n = buf.shape[2]
    blocks = width // LANES
    capacity = own_ref.shape[1]
    me = lax.axis_index(AXIS)
    odd = me % 2 == 1
    before = jnp.maximum(me - 1, 0)
    live_before = jnp.where((me > 0) & jnp.logical_not(odd), live_ref[before], 0)
    live_own = live_ref[me]

    def needs(slot):
        below, chunks = rows_below(prev_ref, slot, before, tile_rows, n)
        return jnp.where(slot < live_before, chunks, 0)

    def load(slot):
        block, _ = place(prev_ref, slot, blocks)
        cols = pl.ds(pl.multiple_of(block * LANES, LANES), 2 * LANES)
        return pltpu.make_async_copy(
            tile_ref.at[:, pl.ds(0, n), cols], buf.at[slot], sems.at[slot]
        )

    @pl.loop(0, live_before)
    def _(slot):
        pl.when(needs(slot) > 0)(load(slot).start)

    total_own = 0
    for slot in range(capacity):
        _, chunks = rows_below(own_ref, slot, me, tile_rows, n)
        total_own += jnp.where(slot < live_own, chunks, 0)

    def pack(slot, first):
        chunks = needs(slot)

        @pl.when(chunks > 0)
        def _():
            load(slot).wait()
            _, shift = place(prev_ref, slot, blocks)
            for p in range(planes):
                rows = window_lanes(buf[slot, p, :, :LANES], buf[slot, p, :, LANES:], shift)
                rows = rows.astype(jnp.bfloat16)
                for c in range(n // CHUNK):
                    packed[first + c, p] = rows[c * CHUNK : (c + 1) * CHUNK]

        return first + chunks

    total_before = lax.fori_loop(0, live_before, pack, 0)
    level = level_of(jnp.where(odd, total_own, total_before), sizes)
    level_ref[0] = level
    for i, size in enumerate(sizes):
        @pl.when((level == i) & (total_before > 0))
        def _():
            store = pltpu.make_async_copy(
                packed.at[pl.ds(0, size)], packed_refs[i], sems.at[capacity]
            )
            store.start()
            store.wait()


def pack(own, prev, live_counts, tile, n):
    planes = tile.shape[0]
    capacity = own.shape[1]
    sizes = level_sizes(capacity * (n // CHUNK))
    level, *packed = pl.pallas_call(
        functools.partial(pack_kernel, sizes),
        out_shape=[jax.ShapeDtypeStruct((1,), jnp.int32)]
        + [jax.ShapeDtypeStruct((size, planes, CHUNK, LANES), jnp.bfloat16) for size in sizes],
        in_specs=[SMEM, SMEM, SMEM, ANY],
        out_specs=[SMEM] + [ANY] * len(sizes),
        scratch_shapes=[
            pltpu.VMEM((capacity, planes, n, 2 * LANES), jnp.bfloat16),
            pltpu.VMEM((sizes[-1] + n // CHUNK, planes, CHUNK, LANES), jnp.bfloat16),
            pltpu.SemaphoreType.DMA((capacity + 1,)),
        ],
        compiler_params=params(12),
        name="pack_rows",
    )(own, prev, live_counts, tile)
    return level[0], packed


def cut_kernel(own_ref, live_ref, tile_ref, win_ref, buf, slab, sems):
    planes, tile_rows, width = tile_ref.shape
    n = win_ref.shape[2]
    blocks = width // LANES
    capacity = own_ref.shape[1]
    tall = n + CHUNK
    me = lax.axis_index(AXIS)
    live = live_ref[me]

    def top(slot):
        row = own_ref[0, slot] - me * tile_rows
        base = jnp.minimum(row // CHUNK * CHUNK, tile_rows - tall)
        return pl.multiple_of(base, CHUNK), row - base

    def load(slot):
        block, _ = place(own_ref, slot, blocks)
        cols = pl.ds(pl.multiple_of(block * LANES, LANES), 2 * LANES)
        base, _ = top(slot)
        return pltpu.make_async_copy(
            tile_ref.at[:, pl.ds(base, tall), cols], buf.at[slot], sems.at[slot]
        )

    @pl.loop(0, live)
    def _(slot):
        load(slot).start()

    @pl.loop(0, capacity)
    def _(slot):
        @pl.when(slot < live)
        def _():
            load(slot).wait()
            _, shift = place(own_ref, slot, blocks)
            _, skip = top(slot)
            table = selector(shift, False)
            for p in range(planes):
                slab[p, pl.ds(0, tall), :] = matmul(buf[slot, p], table)
            for p in range(planes):
                win_ref[slot, p] = slab[p, pl.ds(skip, n), :].astype(jnp.bfloat16)

        @pl.when(slot >= live)
        def _():
            @pl.loop(0, planes)
            def _(p):
                win_ref[slot, p] = jnp.zeros(win_ref.shape[2:], jnp.bfloat16)


def cut(own, live_counts, tile, n):
    planes = tile.shape[0]
    capacity = own.shape[1]
    tall = n + CHUNK
    return pl.pallas_call(
        cut_kernel,
        out_shape=jax.ShapeDtypeStruct((capacity, planes, n, LANES), jnp.bfloat16),
        in_specs=[SMEM, SMEM, ANY],
        out_specs=VMEM,
        scratch_shapes=[
            pltpu.VMEM((capacity, planes, tall, 2 * LANES), jnp.bfloat16),
            pltpu.VMEM((planes, tall + n, LANES), jnp.float32),
            pltpu.SemaphoreType.DMA((capacity,)),
        ],
        compiler_params=params(16),
        cost_estimate=pl.CostEstimate(flops=10**9, bytes_accessed=10**7, transcendentals=0),
        name="cut_windows",
    )(own, live_counts, tile)


def dft_tables(n):
    positions = np.arange(n)
    product = positions[:, None] * positions[None, :] % n
    angles = 2.0 * math.pi / n * product
    real = np.cos(angles) / math.sqrt(n)
    imag = -np.sin(angles) / math.sqrt(n)
    left = np.block([[real, -imag], [imag, real]])
    return (jnp.asarray(left, jnp.bfloat16), jnp.asarray(left.T, jnp.bfloat16))


def stack_rows(fields):
    return jnp.concatenate(
        [jnp.concatenate([re, im], 0).astype(jnp.bfloat16) for re, im in fields], 1
    )


def stack_lanes(fields):
    return jnp.concatenate(
        [jnp.concatenate([re, im], 1).astype(jnp.bfloat16) for re, im in fields], 0
    )


def from_rows(block, n):
    return [(block[:n, k * n : (k + 1) * n], block[n:, k * n : (k + 1) * n]) for k in range(2)]


def from_lanes(block, n):
    return [(block[k * n : (k + 1) * n, :n], block[k * n : (k + 1) * n, n:]) for k in range(2)]


def transform(fields, left, right):
    n = fields[0][0].shape[0]
    out = []
    halfway = [matmul(left, stack_rows(fields[k : k + 2])) for k in range(0, len(fields), 2)]
    for half in halfway:
        out += from_lanes(matmul(stack_lanes(from_rows(half, n)), right), n)
    return out


def transform_back(grads, left, right):
    n = grads[0][0].shape[0]
    out = []
    halfway = [matmul(stack_lanes(grads[k : k + 2]), right) for k in range(0, len(grads), 2)]
    for half in halfway:
        result = matmul(left, stack_rows(from_lanes(half, n)))
        out += from_rows(result.astype(jnp.bfloat16).astype(jnp.float32), n)
    return out


def wave_kernel(
    scale, tile_rows, sizes,
    own_ref, live_ref, next_ref, cross_ref, win_ref,
    probe_ref, cos_ref, sin_ref, fwd_ref, bwd_ref, measured_ref,
    probe_out_ref, grads_ref, *refs,
):
    *packed_refs, below_ref, rims, packed, win, waves, cots, sems = refs
    blocks = next_ref.shape[2] // LANES
    capacity, planes, n, _ = win_ref.shape
    slices = planes // 2
    me = lax.axis_index(AXIS)
    live = live_ref[me]
    odd = me % 2 == 1

    def needs(slot):
        below, chunks = rows_below(own_ref, slot, me, tile_rows, n)
        return below, jnp.where(slot < live, chunks, 0)

    total = 0
    for slot in range(capacity):
        total += needs(slot)[1]

    def load(piece):
        part = pl.ds(piece * PIECE, PIECE)
        return pltpu.make_async_copy(cross_ref.at[part], below_ref.at[part], sems.at[piece])

    def load_rim(slot):
        block, _ = place(own_ref, slot, blocks)
        cols = pl.ds(pl.multiple_of(block * LANES, LANES), 2 * LANES)
        return pltpu.make_async_copy(
            next_ref.at[:, pl.ds(0, n), cols], rims.at[slot], sems.at[slot]
        )

    pieces = jnp.where(odd, (total + PIECE - 1) // PIECE, 0)

    @pl.loop(0, pieces)
    def _(piece):
        load(piece).start()

    @pl.when(jnp.logical_not(odd))
    def _():
        @pl.loop(0, live)
        def _(slot):
            pl.when(needs(slot)[1] > 0)(load_rim(slot).start)

    @pl.loop(0, capacity)
    def _(slot):
        for p in range(planes):
            win[slot, p, pl.ds(0, n), :] = win_ref[slot, p].astype(jnp.float32)

    @pl.loop(0, pieces)
    def _(piece):
        load(piece).wait()

    def fill(slot, first):
        below, chunks = needs(slot)

        @pl.when((chunks > 0) & jnp.logical_not(odd))
        def _():
            load_rim(slot).wait()
            _, shift = place(own_ref, slot, blocks)
            for p in range(planes):
                rows = window_lanes(rims[slot, p, :, :LANES], rims[slot, p, :, LANES:], shift)
                rows = rows.astype(jnp.bfloat16)
                for c in range(n // CHUNK):
                    below_ref[first + c, p] = rows[c * CHUNK : (c + 1) * CHUNK]

        @pl.loop(0, chunks)
        def _(c):
            for p in range(planes):
                win[slot, p, pl.ds(n - below + c * CHUNK, CHUNK), :] = below_ref[
                    first + c, p
                ].astype(jnp.float32)

        return first + chunks

    lax.fori_loop(0, live, fill, 0)

    each = range(capacity)
    ahead, behind = fwd_ref[...], bwd_ref[...]

    def through(k, s):
        w_re, w_im = waves[k, s, 0, :n, :], waves[k, s, 1, :n, :]
        o_re, o_im = win[k, 2 * s, :n, :], win[k, 2 * s + 1, :n, :]
        return (w_re * o_re - w_im * o_im, w_re * o_im + w_im * o_re)

    def through_back(k, s):
        g_re, g_im = cots[k, 0, :n, :], cots[k, 1, :n, :]
        w_re, w_im = waves[k, s, 0, :n, :], waves[k, s, 1, :n, :]
        o_re, o_im = win[k, 2 * s, :n, :], win[k, 2 * s + 1, :n, :]
        d_re = g_re * w_re + g_im * w_im
        d_im = g_im * w_re - g_re * w_im
        win[k, 2 * s, :n, :] = d_re
        win[k, 2 * s + 1, :n, :] = d_im
        grads_ref[k, 2 * s] = d_re.astype(jnp.bfloat16)
        grads_ref[k, 2 * s + 1] = d_im.astype(jnp.bfloat16)
        return (g_re * o_re + g_im * o_im, g_im * o_re - g_re * o_im)

    def keep(ref, k, field):
        ref[0, :n, :] = field[0]
        ref[1, :n, :] = field[1]

    for k in each:
        keep(waves.at[k, 0], k, (probe_ref[0], probe_ref[1]))

    @pl.loop(0, slices - 1)
    def _(s):
        fields = transform([through(k, s) for k in each], ahead, behind)
        h_re, h_im = cos_ref[...], sin_ref[...]
        fields = [(a * h_re - b * h_im, a * h_im + b * h_re) for a, b in fields]
        fields = transform(fields, behind, ahead)
        for k in each:
            keep(waves.at[k, s + 1], k, fields[k])

    fields = transform([through(k, slices - 1) for k in each], ahead, behind)
    for k in each:
        f_re, f_im = fields[k]
        weight = jnp.where(k < live, 2.0, 0.0)
        target = measured_ref[k].astype(jnp.float32)
        inverse = lax.rsqrt(f_re * f_re + f_im * f_im + RIDGE)
        slope = weight * (1.0 - target * inverse)
        fields[k] = (slope * f_re, slope * f_im)
    fields = transform_back(fields, behind, ahead)
    for k in each:
        keep(cots.at[k], k, fields[k])

    @pl.loop(0, slices - 1)
    def _(step):
        s = slices - 1 - step
        fields = transform_back([through_back(k, s) for k in each], ahead, behind)
        h_re, h_im = cos_ref[...], sin_ref[...]
        fields = [(a * h_re + b * h_im, b * h_re - a * h_im) for a, b in fields]
        fields = transform_back(fields, behind, ahead)
        for k in each:
            keep(cots.at[k], k, fields[k])

    fields = [through_back(k, 0) for k in each]
    for part in range(2):
        sum_of = fields[0][part]
        for k in range(1, capacity):
            sum_of = sum_of + fields[k][part]
        probe_out_ref[part] = (sum_of * scale).astype(jnp.bfloat16)

    def hand_on(slot, first):
        below, chunks = needs(slot)

        @pl.when(chunks > 0)
        def _():
            for p in range(planes):
                win[slot, p, pl.ds(n, CHUNK), :] = jnp.zeros((CHUNK, LANES), jnp.float32)

            @pl.loop(0, chunks)
            def _(c):
                for p in range(planes):
                    packed[first + c, p] = win[
                        slot, p, pl.ds(n - below + c * CHUNK, CHUNK), :
                    ].astype(jnp.bfloat16)

        return first + chunks

    lax.fori_loop(0, live, hand_on, 0)
    level = level_of(total, sizes)
    for i, size in enumerate(sizes):
        target = (total > 0) & jnp.where(odd, level == i, size == sizes[-1])

        @pl.when(target)
        def _():
            store = pltpu.make_async_copy(packed.at[pl.ds(0, size)], packed_refs[i], sems.at[0])
            store.start()
            store.wait()


def run_waves(scale, tile_rows, own, live_counts, next_tile, from_cross, win, probe, h_re, h_im, tables, measured):
    capacity, planes, n, _ = win.shape
    sizes = level_sizes(from_cross.shape[0])
    padded = (sizes[-1] + n // CHUNK, planes, CHUNK, LANES)
    probe_part, grads, *packed = pl.pallas_call(
        functools.partial(wave_kernel, scale, tile_rows, sizes),
        out_shape=[
            jax.ShapeDtypeStruct(probe.shape, jnp.bfloat16),
            jax.ShapeDtypeStruct(win.shape, jnp.bfloat16),
        ]
        + [jax.ShapeDtypeStruct((size, planes, CHUNK, LANES), jnp.bfloat16) for size in sizes],
        in_specs=[SMEM] * 2 + [ANY] * 2 + [VMEM] * 7,
        out_specs=[VMEM] * 2 + [ANY] * len(sizes),
        scratch_shapes=[
            pltpu.VMEM(padded, jnp.bfloat16),
            pltpu.VMEM((capacity, planes, n, 2 * LANES), jnp.bfloat16),
            pltpu.VMEM(padded, jnp.bfloat16),
            pltpu.VMEM((capacity, planes, n + CHUNK, LANES), jnp.float32),
            pltpu.VMEM((capacity, planes // 2, 2, n + ROW_PAD, n), jnp.float32),
            pltpu.VMEM((capacity, 2, n + ROW_PAD, n), jnp.float32),
            pltpu.SemaphoreType.DMA((max(capacity, sizes[-1] // PIECE),)),
        ],
        compiler_params=params(36),
        name="waves",
    )(own, live_counts, next_tile, from_cross, win, probe, h_re, h_im, *tables, measured)
    return probe_part, grads, packed


def deposit_kernel(own_ref, live_ref, grads_ref, object_ref, top_ref, acc, sems):
    capacity, planes, n, _ = grads_ref.shape
    tile_rows = object_ref.shape[1]
    blocks = object_ref.shape[2] // LANES
    me = lax.axis_index(AXIS)

    @pl.loop(0, planes)
    def _(p):
        @pl.loop(0, blocks, unroll=2)
        def _(b):
            acc[p, b] = jnp.zeros(acc.shape[2:], jnp.float32)

    @pl.loop(0, live_ref[me])
    def _(slot):
        block, shift = place(own_ref, slot, blocks)
        rows = pl.ds(own_ref[0, slot] - me * tile_rows, n)
        table = selector(shift, True)

        for p in range(planes):
            wide = matmul(grads_ref[slot, p], table)
            acc[p, block, rows, :] += wide[:, :LANES]
            acc[p, block + 1, rows, :] += wide[:, LANES:]

    def stores(b):
        rest = pl.ds(n, tile_rows - n)
        return (
            pltpu.make_async_copy(
                acc.at[:, b, rest, :],
                object_ref.at[:, rest, pl.ds(pl.multiple_of(b * LANES, LANES), LANES)],
                sems.at[b],
            ),
            pltpu.make_async_copy(
                acc.at[:, b, pl.ds(0, n), :], top_ref.at[:, b], sems.at[blocks + b]
            ),
        )

    @pl.loop(0, blocks)
    def _(b):
        for store in stores(b):
            store.start()

    @pl.loop(0, blocks)
    def _(b):
        for store in stores(b):
            store.wait()


def deposit(own, live_counts, grads, tile_rows, width):
    capacity, planes, n, _ = grads.shape
    blocks = width // LANES
    return pl.pallas_call(
        deposit_kernel,
        out_shape=(
            jax.ShapeDtypeStruct((planes, tile_rows, width), jnp.float32),
            jax.ShapeDtypeStruct((planes, blocks, n, LANES), jnp.float32),
        ),
        in_specs=[SMEM, SMEM, VMEM],
        out_specs=(pl.BlockSpec(memory_space=pltpu.HBM), ANY),
        scratch_shapes=[
            pltpu.VMEM((planes, blocks, tile_rows + n, LANES), jnp.float32),
            pltpu.SemaphoreType.DMA((2 * blocks,)),
        ],
        compiler_params=params(54),
        cost_estimate=pl.CostEstimate(flops=10**9, bytes_accessed=10**7, transcendentals=0),
        name="deposit_windows",
    )(own, live_counts, grads)


def finish_kernel(
    prev_ref, live_ref, object_in_ref, top_ref, pair_ref, cross_ref, object_ref, back, acc, sems
):
    planes, blocks, n, _ = acc.shape
    tile_rows = object_ref.shape[1]
    capacity = prev_ref.shape[1]
    first_put = pair_ref.shape[0] // PIECE
    me = lax.axis_index(AXIS)
    odd = me % 2 == 1
    before = jnp.maximum(me - 1, 0)
    live = jnp.where(me > 0, live_ref[before], 0)

    def needs(slot):
        _, chunks = rows_below(prev_ref, slot, before, tile_rows, n)
        return jnp.where(slot < live, chunks, 0)

    total = 0
    for slot in range(capacity):
        total += needs(slot)

    def load(source, piece):
        part = pl.ds(piece * PIECE, PIECE)
        return pltpu.make_async_copy(source.at[part], back.at[part], sems.at[piece])

    pieces = (total + PIECE - 1) // PIECE

    @pl.loop(0, pieces)
    def _(piece):
        pl.when(odd)(load(pair_ref, piece).start)
        pl.when(jnp.logical_not(odd))(load(cross_ref, piece).start)

    def fetch(b):
        return pltpu.make_async_copy(top_ref.at[:, b], acc.at[:, b], sems.at[first_put + b])

    def put(b):
        return pltpu.make_async_copy(
            acc.at[:, b],
            object_ref.at[:, pl.ds(0, n), pl.ds(pl.multiple_of(b * LANES, LANES), LANES)],
            sems.at[first_put + b],
        )

    @pl.loop(0, blocks)
    def _(b):
        fetch(b).start()

    @pl.loop(0, pieces)
    def _(piece):
        load(pair_ref, piece).wait()

    @pl.loop(0, blocks)
    def _(b):
        fetch(b).wait()

    lane = lax.broadcasted_iota(jnp.int32, (CHUNK, LANES), 1)

    def add(slot, first):
        chunks = needs(slot)

        @pl.when(chunks > 0)
        def _():
            block, shift = place(prev_ref, slot, blocks)
            ahead = lax.rem(shift, LANES)
            for p in range(planes):
                for c in range(n // CHUNK):
                    part = pltpu.roll(back[first + c, p].astype(jnp.float32), ahead, 1)
                    part = jnp.where(c < chunks, part, 0.0)
                    rows = pl.ds(c * CHUNK, CHUNK)
                    acc[p, block, rows, :] += jnp.where(lane >= shift, part, 0.0)
                    acc[p, block + 1, rows, :] += jnp.where(lane < shift, part, 0.0)

        return first + chunks

    lax.fori_loop(0, live, add, 0)

    @pl.loop(0, blocks)
    def _(b):
        put(b).start()

    @pl.loop(0, blocks)
    def _(b):
        put(b).wait()


def finish(prev, live_counts, grad, top, from_pair, from_cross):
    planes, blocks, n, _ = top.shape
    hbm = pl.BlockSpec(memory_space=pltpu.HBM)
    chunks = from_pair.shape[0]
    return pl.pallas_call(
        finish_kernel,
        out_shape=jax.ShapeDtypeStruct(grad.shape, grad.dtype),
        in_specs=[SMEM, SMEM, hbm, ANY, ANY, ANY],
        out_specs=hbm,
        input_output_aliases={2: 0},
        scratch_shapes=[
            pltpu.VMEM((chunks + n // CHUNK,) + from_pair.shape[1:], jnp.bfloat16),
            pltpu.VMEM(top.shape, jnp.float32),
            pltpu.SemaphoreType.DMA((chunks // PIECE + 1 + blocks,)),
        ],
        compiler_params=params(50),
        cost_estimate=pl.CostEstimate(flops=10**9, bytes_accessed=2 * 10**7, transcendentals=0),
        name="add_from_before",
    )(prev, live_counts, grad, top, from_pair, from_cross)


def local(transmission, probe_wavefield, phase_shift, offsets, live_counts, measured):
    slices, parts, tile_rows, width = transmission.shape
    n = probe_wavefield.shape[-1]
    capacity = offsets.shape[1]
    devices = lax.axis_size(AXIS)
    tile = transmission.reshape(slices * parts, tile_rows, width)
    prev = lax.ppermute(offsets, AXIS, [(i, i + 1) for i in range(devices - 1)])
    phase = (jnp.cos(phase_shift), jnp.sin(phase_shift))
    prev, behind_prev, *phase = lax.optimization_barrier((prev, tile, *phase))
    next_tile = within_pair(behind_prev, False)
    level, packed = pack(offsets, prev, live_counts, tile, n)
    from_cross, win = between_pairs_upto(
        level, packed, False,
        lambda own, live, tile: cut(own, live, tile, n),
        (offsets, live_counts, tile),
    )
    scale = 1.0 / math.sqrt(capacity * devices)
    probe_part, grads, packed = run_waves(
        scale, tile_rows, offsets, live_counts, next_tile, from_cross, win,
        probe_wavefield, *phase, dft_tables(n), measured,
    )
    back_pair = within_pair(packed[-1], True)
    shares = scattered(probe_part)
    back_cross, (grad, top) = between_pairs_upto(
        level, packed, True,
        lambda own, live, grads: deposit(own, live, grads, tile_rows, width),
        (offsets, live_counts, grads),
    )
    probe_grad = lax.all_to_all(summed_shares(shares, top), AXIS, 0, 0)
    grad = finish(prev, live_counts, grad, top, back_pair, back_cross)
    probe_grad, grad = lax.optimization_barrier((probe_grad, grad))
    probe_grad = probe_grad.reshape(probe_wavefield.shape).astype(jnp.float32)
    return (grad.reshape(slices, parts, tile_rows, width), probe_grad)


def solution(mesh):
    in_specs = (
        P(None, None, ("groups", "ty"), None),
        P("groups", None, None),
        P(),
        P(None, ("groups", "ty")),
        P("groups"),
        P(("groups", "ty"), None, None),
    )
    out_specs = (P(None, None, ("groups", "ty"), None), P("groups", None, None))
    return jax.shard_map(local, mesh=mesh, in_specs=in_specs, out_specs=out_specs, check_vma=False)
```

```python
import functools
import math

import jax
import jax.numpy as jnp
import numpy as np
from jax import lax
from jax.experimental import pallas as pl
from jax.experimental.pallas import tpu as pltpu
from jax.sharding import PartitionSpec as P

RIDGE = 0.25
LANES = 128
CHUNK = 16
PIECE = 8
ROW_PAD = 8
AXIS = "ty"

ANY = pl.BlockSpec(memory_space=pl.ANY)
VMEM = pl.BlockSpec(memory_space=pltpu.VMEM)
SMEM = pl.BlockSpec(memory_space=pltpu.SMEM)


def params(mib):
    return pltpu.CompilerParams(vmem_limit_bytes=mib * 2**20)


def matmul(a, b):
    return jnp.dot(a, b, preferred_element_type=jnp.float32)


def within_pair(block, up):
    devices = lax.axis_size(AXIS)
    pairs = [(i + 1, i) for i in range(0, devices - 1, 2)]
    if up:
        pairs = [(b, a) for a, b in pairs]
    return lax.ppermute(block, AXIS, pairs)


def between_pairs(block, up):
    devices = lax.axis_size(AXIS)
    pairs = [(i + 1, i) for i in range(1, devices - 1, 2)]
    if up:
        pairs = [(b, a) for a, b in pairs]
    return lax.ppermute(block, AXIS, pairs)


def level_sizes(chunks):
    return (3 * chunks // 8, chunks // 2, 5 * chunks // 8, chunks)


def level_of(total, sizes):
    level = 0
    for size in sizes[:-1]:
        level += jnp.where(total > size, 1, 0)
    return level


def place_kernel(source_ref, target_ref, sem):
    copy = pltpu.make_async_copy(source_ref, target_ref.at[pl.ds(0, source_ref.shape[0])], sem)
    copy.start()
    copy.wait()


def placed(block, shape):
    return pl.pallas_call(
        place_kernel,
        out_shape=jax.ShapeDtypeStruct(shape, block.dtype),
        in_specs=[ANY],
        out_specs=ANY,
        scratch_shapes=[pltpu.SemaphoreType.DMA],
        compiler_params=params(2),
        name="place_chunks",
    )(block)


def between_pairs_upto(level, packed, up, beside, operands):
    full = packed[-1].shape

    def branch(i):
        def run(packed, *operands):
            got = between_pairs(packed[i], up)
            other = beside(*operands)
            if got.shape != full:
                got = placed(got, full)
            return got, other

        return run

    return lax.switch(level, [branch(i) for i in range(len(packed))], packed, *operands)


def idle_kernel(out_ref):
    del out_ref


def rest_of_pair(over, packed, up):
    def none(packed):
        return pl.pallas_call(
            idle_kernel,
            out_shape=jax.ShapeDtypeStruct(packed.shape, packed.dtype),
            out_specs=ANY,
            compiler_params=params(2),
            name="no_rest",
        )()

    return lax.cond(over > 0, lambda packed: within_pair(packed, up), none, packed)


def sum_kernel(count, *refs):
    terms = [ref[...].astype(jnp.float32) for ref in refs[:count]]
    if count == 2:
        total = terms[0] + terms[1]
    else:
        total = (terms[0] + terms[1]) + (terms[2] + terms[3])
    out_ref = refs[-1]
    out_ref[...] = total.astype(out_ref.dtype)


def exchange(block, steps):
    devices = lax.axis_size(AXIS)
    return [block] + [lax.ppermute(block, AXIS, [(i, i ^ s) for i in range(devices)]) for s in steps]


def summed(terms, dtype, after=()):
    return pl.pallas_call(
        functools.partial(sum_kernel, len(terms)),
        out_shape=jax.ShapeDtypeStruct(terms[0].shape, dtype),
        in_specs=[VMEM] * len(terms) + [ANY] * len(after),
        out_specs=VMEM,
        compiler_params=params(4),
        name="sum_partners",
    )(*terms, *after)


def exchange_rounds(devices):
    rounds = []
    step = 1
    while step < devices:
        if step * 2 < devices:
            rounds.append((step, 2 * step, 3 * step))
        else:
            rounds.append((step,))
        step *= 4
    return rounds[::-1]


def place(offsets_ref, slot, blocks):
    col = offsets_ref[1, slot]
    block = jnp.minimum(col // LANES, blocks - 2)
    return block, col - block * LANES


def rows_below(offsets_ref, slot, owner, tile_rows, n):
    below = jnp.maximum(offsets_ref[0, slot] - owner * tile_rows + n - tile_rows, 0)
    return below, (below + CHUNK - 1) // CHUNK


def hand_over(within, level, total, sizes, packed, packed_refs, sem):
    for i, size in enumerate(sizes):
        first = 0
        if i == 0:
            wanted = jnp.where(within, total > 0, (level == i) & (total > 0))
        elif i == len(sizes) - 2:
            first = jnp.where(within, sizes[0], 0)
            wanted = jnp.where(within, total > sizes[0], level == i)
        else:
            wanted = jnp.logical_not(within) & (level == i)

        @pl.when(wanted)
        def _():
            store = pltpu.make_async_copy(packed.at[pl.ds(first, size)], packed_refs[i], sem)
            store.start()
            store.wait()


def load_below(within, pair_ref, rest_ref, cross_ref, target, sems, pieces, run):
    first = pair_ref.shape[0] // PIECE

    @pl.loop(0, pieces)
    def _(piece):
        part = pl.ds(piece * PIECE, PIECE)
        rest = pl.ds((piece - first) * PIECE, PIECE)
        for wanted, source, where in (
            (jnp.logical_not(within), cross_ref, part),
            (within & (piece < first), pair_ref, part),
            (within & (piece >= first), rest_ref, rest),
        ):
            @pl.when(wanted)
            def _():
                run(pltpu.make_async_copy(source.at[where], target.at[part], sems.at[piece]))


def window_lanes(left, right, shift):
    lane = lax.broadcasted_iota(jnp.int32, left.shape, 1)
    back = lax.rem(LANES - shift, LANES)
    left = pltpu.roll(left.astype(jnp.float32), back, 1)
    right = pltpu.roll(right.astype(jnp.float32), back, 1)
    return jnp.where(lane < LANES - shift, left, right)


def selector(shift, transposed):
    shape = (LANES, 2 * LANES) if transposed else (2 * LANES, LANES)
    wide = lax.broadcasted_iota(jnp.int32, shape, 1 if transposed else 0)
    narrow = lax.broadcasted_iota(jnp.int32, shape, 0 if transposed else 1)
    return jnp.where(wide == narrow + shift, 1.0, 0.0).astype(jnp.bfloat16)


def pack_kernel(sizes, own_ref, prev_ref, live_ref, tile_ref, *refs):
    level_ref, over_ref, *packed_refs, buf, packed, sems = refs
    planes, tile_rows, width = tile_ref.shape
    n = buf.shape[2]
    blocks = width // LANES
    capacity = own_ref.shape[1]
    me = lax.axis_index(AXIS)
    odd = me % 2 == 1
    before = jnp.maximum(me - 1, 0)
    live_before = jnp.where(me > 0, live_ref[before], 0)
    live_own = live_ref[me]

    def needs(slot):
        below, chunks = rows_below(prev_ref, slot, before, tile_rows, n)
        return jnp.where(slot < live_before, chunks, 0)

    def load(slot):
        block, _ = place(prev_ref, slot, blocks)
        cols = pl.ds(pl.multiple_of(block * LANES, LANES), 2 * LANES)
        return pltpu.make_async_copy(
            tile_ref.at[:, pl.ds(0, n), cols], buf.at[slot], sems.at[slot]
        )

    @pl.loop(0, live_before)
    def _(slot):
        pl.when(needs(slot) > 0)(load(slot).start)

    total_own = 0
    for slot in range(capacity):
        _, chunks = rows_below(own_ref, slot, me, tile_rows, n)
        total_own += jnp.where(slot < live_own, chunks, 0)

    def pack(slot, first):
        chunks = needs(slot)

        @pl.when(chunks > 0)
        def _():
            load(slot).wait()
            _, shift = place(prev_ref, slot, blocks)
            for p in range(planes):
                rows = window_lanes(buf[slot, p, :, :LANES], buf[slot, p, :, LANES:], shift)
                rows = rows.astype(jnp.bfloat16)
                for c in range(n // CHUNK):
                    packed[first + c, p] = rows[c * CHUNK : (c + 1) * CHUNK]

        return first + chunks

    total_before = lax.fori_loop(0, live_before, pack, 0)
    level = level_of(jnp.where(odd, total_own, total_before), sizes)
    level_ref[0] = level
    over_ref[0] = jnp.where(jnp.where(odd, total_before, total_own) > sizes[0], 1, 0)
    hand_over(odd, level, total_before, sizes, packed, packed_refs, sems.at[capacity])


def pack(own, prev, live_counts, tile, n):
    planes = tile.shape[0]
    capacity = own.shape[1]
    sizes = level_sizes(capacity * (n // CHUNK))
    level, over, *packed = pl.pallas_call(
        functools.partial(pack_kernel, sizes),
        out_shape=[jax.ShapeDtypeStruct((1,), jnp.int32)] * 2
        + [jax.ShapeDtypeStruct((size, planes, CHUNK, LANES), jnp.bfloat16) for size in sizes],
        in_specs=[SMEM, SMEM, SMEM, ANY],
        out_specs=[SMEM] * 2 + [ANY] * len(sizes),
        scratch_shapes=[
            pltpu.VMEM((capacity, planes, n, 2 * LANES), jnp.bfloat16),
            pltpu.VMEM((sizes[-1] + n // CHUNK, planes, CHUNK, LANES), jnp.bfloat16),
            pltpu.SemaphoreType.DMA((capacity + 1,)),
        ],
        compiler_params=params(12),
        name="pack_rows",
    )(own, prev, live_counts, tile)
    return level[0], over[0], packed


def cut_kernel(
    own_ref, live_ref, tile_ref, phase_ref, win_ref, cos_ref, sin_ref, buf, slab, sems
):
    planes, tile_rows, width = tile_ref.shape
    n = win_ref.shape[2]
    blocks = width // LANES
    capacity = own_ref.shape[1]
    tall = n + CHUNK
    me = lax.axis_index(AXIS)
    live = live_ref[me]

    def top(slot):
        row = own_ref[0, slot] - me * tile_rows
        base = jnp.minimum(row // CHUNK * CHUNK, tile_rows - tall)
        return pl.multiple_of(base, CHUNK), row - base

    def load(slot):
        block, _ = place(own_ref, slot, blocks)
        cols = pl.ds(pl.multiple_of(block * LANES, LANES), 2 * LANES)
        base, _ = top(slot)
        return pltpu.make_async_copy(
            tile_ref.at[:, pl.ds(base, tall), cols], buf.at[slot], sems.at[slot]
        )

    @pl.loop(0, live)
    def _(slot):
        load(slot).start()

    cos_ref[...] = jnp.cos(phase_ref[...])
    sin_ref[...] = jnp.sin(phase_ref[...])

    @pl.loop(0, capacity)
    def _(slot):
        @pl.when(slot < live)
        def _():
            load(slot).wait()
            _, shift = place(own_ref, slot, blocks)
            _, skip = top(slot)
            table = selector(shift, False)
            for p in range(planes):
                slab[p, pl.ds(0, tall), :] = matmul(buf[slot, p], table)
            for p in range(planes):
                win_ref[slot, p] = slab[p, pl.ds(skip, n), :].astype(jnp.bfloat16)

        @pl.when(slot >= live)
        def _():
            @pl.loop(0, planes)
            def _(p):
                win_ref[slot, p] = jnp.zeros(win_ref.shape[2:], jnp.bfloat16)


def cut(own, live_counts, tile, phase):
    planes = tile.shape[0]
    n = phase.shape[0]
    capacity = own.shape[1]
    tall = n + CHUNK
    return pl.pallas_call(
        cut_kernel,
        out_shape=(
            jax.ShapeDtypeStruct((capacity, planes, n, LANES), jnp.bfloat16),
            jax.ShapeDtypeStruct(phase.shape, phase.dtype),
            jax.ShapeDtypeStruct(phase.shape, phase.dtype),
        ),
        in_specs=[SMEM, SMEM, ANY, VMEM],
        out_specs=(VMEM,) * 3,
        scratch_shapes=[
            pltpu.VMEM((capacity, planes, tall, 2 * LANES), jnp.bfloat16),
            pltpu.VMEM((planes, tall + n, LANES), jnp.float32),
            pltpu.SemaphoreType.DMA((capacity,)),
        ],
        compiler_params=params(16),
        cost_estimate=pl.CostEstimate(flops=10**9, bytes_accessed=10**7, transcendentals=0),
        name="cut_windows",
    )(own, live_counts, tile, phase)


def dft_tables(n):
    positions = np.arange(n)
    product = positions[:, None] * positions[None, :] % n
    angles = 2.0 * math.pi / n * product
    real = np.cos(angles) / math.sqrt(n)
    imag = -np.sin(angles) / math.sqrt(n)
    left = np.block([[real, -imag], [imag, real]])
    return (jnp.asarray(left, jnp.bfloat16), jnp.asarray(left.T, jnp.bfloat16))


def stack_rows(fields):
    return jnp.concatenate(
        [jnp.concatenate([re, im], 0).astype(jnp.bfloat16) for re, im in fields], 1
    )


def stack_lanes(fields):
    return jnp.concatenate(
        [jnp.concatenate([re, im], 1).astype(jnp.bfloat16) for re, im in fields], 0
    )


def from_rows(block, n):
    return [(block[:n, k * n : (k + 1) * n], block[n:, k * n : (k + 1) * n]) for k in range(2)]


def from_lanes(block, n):
    return [(block[k * n : (k + 1) * n, :n], block[k * n : (k + 1) * n, n:]) for k in range(2)]


def transform(fields, left, right):
    n = fields[0][0].shape[0]
    out = []
    halfway = [matmul(left, stack_rows(fields[k : k + 2])) for k in range(0, len(fields), 2)]
    for half in halfway:
        out += from_lanes(matmul(stack_lanes(from_rows(half, n)), right), n)
    return out


def transform_back(grads, left, right):
    n = grads[0][0].shape[0]
    out = []
    halfway = [matmul(stack_lanes(grads[k : k + 2]), right) for k in range(0, len(grads), 2)]
    for half in halfway:
        result = matmul(left, stack_rows(from_lanes(half, n)))
        out += from_rows(result.astype(jnp.bfloat16).astype(jnp.float32), n)
    return out


def wave_kernel(
    scale, tile_rows, sizes,
    own_ref, live_ref, pair_ref, rest_ref, cross_ref, win_ref,
    probe_ref, cos_ref, sin_ref, fwd_ref, bwd_ref, measured_ref,
    probe_out_ref, grads_out_ref, *refs,
):
    *packed_refs, below_ref, packed, win_in, grads_ref, win, waves, cots, sems, win_sems, grad_sems = refs
    capacity, planes, n, _ = win_ref.shape
    slices = planes // 2
    me = lax.axis_index(AXIS)
    live = live_ref[me]
    odd = me % 2 == 1

    def needs(slot):
        below, chunks = rows_below(own_ref, slot, me, tile_rows, n)
        return below, jnp.where(slot < live, chunks, 0)

    def load_window(slot):
        return pltpu.make_async_copy(win_ref.at[slot], win_in.at[slot], win_sems.at[slot])

    def store_grads(s):
        part = pl.ds(2 * s, 2)
        return pltpu.make_async_copy(
            grads_ref.at[:, part], grads_out_ref.at[:, part], grad_sems.at[s]
        )

    @pl.loop(0, capacity)
    def _(slot):
        load_window(slot).start()

    total = 0
    for slot in range(capacity):
        total += needs(slot)[1]
    pieces = (total + PIECE - 1) // PIECE
    received = (jnp.logical_not(odd), pair_ref, rest_ref, cross_ref, below_ref, sems, pieces)
    load_below(*received, lambda copy: copy.start())

    @pl.loop(0, capacity)
    def _(slot):
        load_window(slot).wait()
        for p in range(planes):
            win[slot, p, pl.ds(0, n), :] = win_in[slot, p].astype(jnp.float32)

    load_below(*received, lambda copy: copy.wait())

    def fill(slot, first):
        below, chunks = needs(slot)

        @pl.loop(0, chunks)
        def _(c):
            for p in range(planes):
                win[slot, p, pl.ds(n - below + c * CHUNK, CHUNK), :] = below_ref[
                    first + c, p
                ].astype(jnp.float32)

        return first + chunks

    lax.fori_loop(0, live, fill, 0)

    each = range(capacity)
    ahead, behind = fwd_ref[...], bwd_ref[...]

    def through(k, s):
        w_re, w_im = waves[k, s, 0, :n, :], waves[k, s, 1, :n, :]
        o_re, o_im = win[k, 2 * s, :n, :], win[k, 2 * s + 1, :n, :]
        return (w_re * o_re - w_im * o_im, w_re * o_im + w_im * o_re)

    def through_back(k, s):
        g_re, g_im = cots[k, 0, :n, :], cots[k, 1, :n, :]
        w_re, w_im = waves[k, s, 0, :n, :], waves[k, s, 1, :n, :]
        o_re, o_im = win[k, 2 * s, :n, :], win[k, 2 * s + 1, :n, :]
        d_re = g_re * w_re + g_im * w_im
        d_im = g_im * w_re - g_re * w_im
        win[k, 2 * s, :n, :] = d_re
        win[k, 2 * s + 1, :n, :] = d_im
        grads_ref[k, 2 * s] = d_re.astype(jnp.bfloat16)
        grads_ref[k, 2 * s + 1] = d_im.astype(jnp.bfloat16)
        return (g_re * o_re + g_im * o_im, g_im * o_re - g_re * o_im)

    def keep(ref, k, field):
        ref[0, :n, :] = field[0]
        ref[1, :n, :] = field[1]

    for k in each:
        keep(waves.at[k, 0], k, (probe_ref[0], probe_ref[1]))

    @pl.loop(0, slices - 1)
    def _(s):
        fields = transform([through(k, s) for k in each], ahead, behind)
        h_re, h_im = cos_ref[...], sin_ref[...]
        fields = [(a * h_re - b * h_im, a * h_im + b * h_re) for a, b in fields]
        fields = transform(fields, behind, ahead)
        for k in each:
            keep(waves.at[k, s + 1], k, fields[k])

    fields = transform([through(k, slices - 1) for k in each], ahead, behind)
    for k in each:
        f_re, f_im = fields[k]
        weight = jnp.where(k < live, 2.0, 0.0)
        target = measured_ref[k].astype(jnp.float32)
        inverse = lax.rsqrt(f_re * f_re + f_im * f_im + RIDGE)
        slope = weight * (1.0 - target * inverse)
        fields[k] = (slope * f_re, slope * f_im)
    fields = transform_back(fields, behind, ahead)
    for k in each:
        keep(cots.at[k], k, fields[k])

    @pl.loop(0, slices - 1)
    def _(step):
        s = slices - 1 - step
        products = [through_back(k, s) for k in each]
        store_grads(s).start()
        fields = transform_back(products, ahead, behind)
        h_re, h_im = cos_ref[...], sin_ref[...]
        fields = [(a * h_re + b * h_im, b * h_re - a * h_im) for a, b in fields]
        fields = transform_back(fields, behind, ahead)
        for k in each:
            keep(cots.at[k], k, fields[k])

    fields = [through_back(k, 0) for k in each]
    store_grads(0).start()
    for part in range(2):
        sum_of = fields[0][part]
        for k in range(1, capacity):
            sum_of = sum_of + fields[k][part]
        probe_out_ref[part] = (sum_of * scale).astype(jnp.bfloat16)

    def hand_on(slot, first):
        below, chunks = needs(slot)

        @pl.when(chunks > 0)
        def _():
            for p in range(planes):
                win[slot, p, pl.ds(n, CHUNK), :] = jnp.zeros((CHUNK, LANES), jnp.float32)

            @pl.loop(0, chunks)
            def _(c):
                for p in range(planes):
                    packed[first + c, p] = win[
                        slot, p, pl.ds(n - below + c * CHUNK, CHUNK), :
                    ].astype(jnp.bfloat16)

        return first + chunks

    lax.fori_loop(0, live, hand_on, 0)
    level = level_of(total, sizes)
    hand_over(jnp.logical_not(odd), level, total, sizes, packed, packed_refs, sems.at[0])

    @pl.loop(0, slices)
    def _(s):
        store_grads(s).wait()


def run_waves(scale, tile_rows, own, live_counts, received, win, probe, phase, tables, measured):
    capacity, planes, n, _ = win.shape
    chunks = received[-1].shape[0]
    sizes = level_sizes(chunks)
    probe_part, grads, *packed = pl.pallas_call(
        functools.partial(wave_kernel, scale, tile_rows, sizes),
        out_shape=[
            jax.ShapeDtypeStruct(probe.shape, jnp.bfloat16),
            jax.ShapeDtypeStruct(win.shape, jnp.bfloat16),
        ]
        + [jax.ShapeDtypeStruct((size, planes, CHUNK, LANES), jnp.bfloat16) for size in sizes],
        in_specs=[SMEM] * 2 + [ANY] * 4 + [VMEM] * 6,
        out_specs=[VMEM, ANY] + [ANY] * len(sizes),
        scratch_shapes=[
            pltpu.VMEM((chunks, planes, CHUNK, LANES), jnp.bfloat16),
            pltpu.VMEM((chunks, planes, CHUNK, LANES), jnp.bfloat16),
            pltpu.VMEM(win.shape, jnp.bfloat16),
            pltpu.VMEM(win.shape, jnp.bfloat16),
            pltpu.VMEM((capacity, planes, n + CHUNK, LANES), jnp.float32),
            pltpu.VMEM((capacity, planes // 2, 2, n + ROW_PAD, n), jnp.float32),
            pltpu.VMEM((capacity, 2, n + ROW_PAD, n), jnp.float32),
            pltpu.SemaphoreType.DMA((chunks // PIECE,)),
            pltpu.SemaphoreType.DMA((capacity,)),
            pltpu.SemaphoreType.DMA((planes // 2,)),
        ],
        compiler_params=params(26),
        name="waves",
    )(own, live_counts, *received, win, probe, *phase, *tables, measured)
    return probe_part, grads, packed


def deposit_kernel(own_ref, live_ref, grads_ref, object_ref, top_ref, acc, sems):
    capacity, planes, n, _ = grads_ref.shape
    tile_rows = object_ref.shape[1]
    blocks = object_ref.shape[2] // LANES
    me = lax.axis_index(AXIS)

    @pl.loop(0, planes)
    def _(p):
        @pl.loop(0, blocks, unroll=2)
        def _(b):
            acc[p, b] = jnp.zeros(acc.shape[2:], jnp.float32)

    @pl.loop(0, live_ref[me])
    def _(slot):
        block, shift = place(own_ref, slot, blocks)
        rows = pl.ds(own_ref[0, slot] - me * tile_rows, n)
        table = selector(shift, True)

        for p in range(planes):
            wide = matmul(grads_ref[slot, p], table)
            acc[p, block, rows, :] += wide[:, :LANES]
            acc[p, block + 1, rows, :] += wide[:, LANES:]

    def stores(b):
        cols = pl.ds(pl.multiple_of(b * LANES, LANES), LANES)
        return (
            pltpu.make_async_copy(
                acc.at[:, b, pl.ds(0, tile_rows), :], object_ref.at[:, :, cols], sems.at[b]
            ),
            pltpu.make_async_copy(
                acc.at[:, b, pl.ds(0, n), :], top_ref.at[:, b], sems.at[blocks + b]
            ),
        )

    @pl.loop(0, blocks)
    def _(b):
        for store in stores(b):
            store.start()

    @pl.loop(0, blocks)
    def _(b):
        for store in stores(b):
            store.wait()


def deposit(own, live_counts, grads, tile_rows, width):
    capacity, planes, n, _ = grads.shape
    blocks = width // LANES
    return pl.pallas_call(
        deposit_kernel,
        out_shape=(
            jax.ShapeDtypeStruct((planes, tile_rows, width), jnp.float32),
            jax.ShapeDtypeStruct((planes, blocks, n, LANES), jnp.float32),
        ),
        in_specs=[SMEM, SMEM, VMEM],
        out_specs=(pl.BlockSpec(memory_space=pltpu.HBM), ANY),
        scratch_shapes=[
            pltpu.VMEM((planes, blocks, tile_rows + n, LANES), jnp.float32),
            pltpu.SemaphoreType.DMA((2 * blocks,)),
        ],
        compiler_params=params(54),
        cost_estimate=pl.CostEstimate(flops=10**9, bytes_accessed=10**7, transcendentals=0),
        name="deposit_windows",
    )(own, live_counts, grads)


def finish_kernel(
    prev_ref, live_ref, object_in_ref, top_ref, pair_ref, rest_ref, cross_ref,
    object_ref, back, acc, sems, block_sems,
):
    planes, blocks, n, _ = acc.shape
    tile_rows = object_ref.shape[1]
    capacity = prev_ref.shape[1]
    me = lax.axis_index(AXIS)
    odd = me % 2 == 1
    before = jnp.maximum(me - 1, 0)
    live = jnp.where(me > 0, live_ref[before], 0)

    def needs(slot):
        _, chunks = rows_below(prev_ref, slot, before, tile_rows, n)
        return jnp.where(slot < live, chunks, 0)

    total = 0
    touched = 0
    for slot in range(capacity):
        chunks = needs(slot)
        block, _ = place(prev_ref, slot, blocks)
        total += chunks
        touched |= jnp.where(chunks > 0, jnp.left_shift(3, block), 0)
    pieces = (total + PIECE - 1) // PIECE

    def fetch(b):
        return pltpu.make_async_copy(top_ref.at[:, b], acc.at[:, b], block_sems.at[b])

    def put(b):
        cols = pl.ds(pl.multiple_of(b * LANES, LANES), LANES)
        return pltpu.make_async_copy(
            acc.at[:, b], object_ref.at[:, pl.ds(0, n), cols], block_sems.at[b]
        )

    def for_touched(run):
        @pl.loop(0, blocks)
        def _(b):
            @pl.when(jnp.bitwise_and(jnp.right_shift(touched, b), 1) == 1)
            def _():
                run(b)

    received = (odd, pair_ref, rest_ref, cross_ref, back, sems, pieces)
    for_touched(lambda b: fetch(b).start())
    load_below(*received, lambda copy: copy.start())
    load_below(*received, lambda copy: copy.wait())
    for_touched(lambda b: fetch(b).wait())
    lane = lax.broadcasted_iota(jnp.int32, (CHUNK, LANES), 1)

    def add(slot, first):
        chunks = needs(slot)

        @pl.when(chunks > 0)
        def _():
            block, shift = place(prev_ref, slot, blocks)
            ahead = lax.rem(shift, LANES)
            for p in range(planes):
                for c in range(n // CHUNK):
                    part = pltpu.roll(back[first + c, p].astype(jnp.float32), ahead, 1)
                    part = jnp.where(c < chunks, part, 0.0)
                    rows = pl.ds(c * CHUNK, CHUNK)
                    acc[p, block, rows, :] += jnp.where(lane >= shift, part, 0.0)
                    acc[p, block + 1, rows, :] += jnp.where(lane < shift, part, 0.0)

        return first + chunks

    lax.fori_loop(0, live, add, 0)
    for_touched(lambda b: put(b).start())
    for_touched(lambda b: put(b).wait())


def finish(prev, live_counts, grad, top, received):
    planes, blocks, n, _ = top.shape
    hbm = pl.BlockSpec(memory_space=pltpu.HBM)
    chunks = received[-1].shape[0]
    return pl.pallas_call(
        finish_kernel,
        out_shape=jax.ShapeDtypeStruct(grad.shape, grad.dtype),
        in_specs=[SMEM, SMEM, hbm, ANY, ANY, ANY, ANY],
        out_specs=hbm,
        input_output_aliases={2: 0},
        scratch_shapes=[
            pltpu.VMEM((chunks + n // CHUNK,) + received[-1].shape[1:], jnp.bfloat16),
            pltpu.VMEM(top.shape, jnp.float32),
            pltpu.SemaphoreType.DMA((chunks // PIECE,)),
            pltpu.SemaphoreType.DMA((blocks,)),
        ],
        compiler_params=params(50),
        cost_estimate=pl.CostEstimate(flops=10**9, bytes_accessed=2 * 10**7, transcendentals=0),
        name="add_from_before",
    )(prev, live_counts, grad, top, *received)


def local(transmission, probe_wavefield, phase_shift, offsets, live_counts, measured):
    slices, parts, tile_rows, width = transmission.shape
    n = probe_wavefield.shape[-1]
    capacity = offsets.shape[1]
    devices = lax.axis_size(AXIS)
    tile = transmission.reshape(slices * parts, tile_rows, width)
    prev = lax.ppermute(offsets, AXIS, [(i, i + 1) for i in range(devices - 1)])
    level, over, packed = pack(offsets, prev, live_counts, tile, n)
    from_pair = within_pair(packed[0], False)
    from_cross, (win, *phase) = between_pairs_upto(
        level, packed, False, cut, (offsets, live_counts, tile, phase_shift)
    )
    from_cross, over = lax.optimization_barrier((from_cross, over))
    received = (from_pair, rest_of_pair(over, packed[2], False), from_cross)
    scale = 1.0 / math.sqrt(capacity * devices)
    probe_part, grads, packed = run_waves(
        scale, tile_rows, offsets, live_counts, received, win,
        probe_wavefield, phase, dft_tables(n), measured,
    )
    rounds = exchange_rounds(devices)
    back_pair = within_pair(packed[0], True)
    terms = exchange(probe_part, rounds[0])
    back_cross, (grad, top) = between_pairs_upto(
        level, packed, True,
        lambda own, live, grads: deposit(own, live, grads, tile_rows, width),
        (offsets, live_counts, grads),
    )
    for i, steps in enumerate(rounds[1:]):
        terms = exchange(summed(terms, jnp.bfloat16, (top,) if i == 0 else ()), steps)
    back_cross, over = lax.optimization_barrier((back_cross, over))
    received = (back_pair, rest_of_pair(over, packed[2], True), back_cross)
    grad = finish(prev, live_counts, grad, top, received)
    probe_grad = summed(terms, jnp.float32, (grad,))
    return (grad.reshape(slices, parts, tile_rows, width), probe_grad)


def solution(mesh):
    in_specs = (
        P(None, None, ("groups", "ty"), None),
        P("groups", None, None),
        P(),
        P(None, ("groups", "ty")),
        P("groups"),
        P(("groups", "ty"), None, None),
    )
    out_specs = (P(None, None, ("groups", "ty"), None), P("groups", None, None))
    return jax.shard_map(local, mesh=mesh, in_specs=in_specs, out_specs=out_specs, check_vma=False)
```
